32 devices in a mesh: scen: 4 (over y, x), fac: 8 (over z, core).
Axes of the slice: x: 2, y: 2, z: 4, core: 2. Of those that a mesh axis runs over, the one named last changes fastest.
Arguments:
- loadings: bfloat16 [8192, 1000], P('fac'), may hold values from -0.1875 to 0.1875
- reduced_shocks: bfloat16 [1000, 256], P(None, 'scen'), may hold values from -6 to 6
- sensitivity: bfloat16 [8192, 200], P('fac'), may hold values from -0.0625 to 0.0625
- cross_gamma: bfloat16 [16, 1024, 1024], P('fac'), may hold values from -0.005859375 to 0.005859375
- block_list: int32 [12, 3], replicated, may hold values from 0 to 199, as said below
- block_owner: int32 [12], replicated, may hold values from 0 to 7, as said below
- desk_owner: int32 [200], replicated, may hold values from 0 to 7, as said below
- buckets: int32 [8192], replicated, may hold values from 0 to 4
Outputs:
- desk_profit: float32 [208, 5, 256], P('fac', None, 'scen')
- shortfall: float32 [208, 5], P('fac')
- adjusted_es: float32 [208], P('fac')
The draws below stay inside these ranges and needn't reach their ends.
Inputs may be any that keep to these rules, and one draw needn't show every extreme that they name: `block_list`: each row is (row block, column block, desk): block numbers below 8, desks below 200; the fac index holding the row block, and the one holding the column block, is at most two away from the block's owner. `block_owner`: no fac index owns more than 2 blocks; some index owns exactly 2. `desk_owner`: no fac index owns more than 26 desks; some index owns exactly 26.
All inputs are finite; a program needn't handle non-finite values.
Results may differ from the reference program's by a relative error of at most 0.0032.
Values may be sent and summed in bfloat16 or wider, within the bound.
A program may use at most 64 MiB of HBM per device.

```python
import jax
import jax.numpy as jnp
from jax import lax

K = 1000
BLK = 1024
DESKS = 200
HORIZONS = 5
F_DEV = 1024
CAP = 2
FACTORS = 8192
SCEN = 256
BLOCKS = 12
DESK_DEV = 26
DESK_SLOTS = 208
TAIL = 7
N_FAC = 8


def spread_owners(key, slots_each, chosen_count):
    subkeys = jax.random.split(key, 3)
    heavy_device = jax.random.randint(subkeys[0], (), 0, N_FAC)
    order_score = jax.random.permutation(subkeys[1], N_FAC * slots_each).astype(jnp.int32) + 1
    device_of = jnp.arange(N_FAC * slots_each, dtype=jnp.int32) // slots_each
    scores = jnp.where(device_of == heavy_device, 0, order_score)
    chosen = jnp.argsort(scores, stable=True)[:chosen_count]
    chosen = chosen[jax.random.permutation(subkeys[2], chosen_count)]
    return (chosen // slots_each).astype(jnp.int32)


def block_plan(key):
    base = jax.random.fold_in(key, 11)
    subkeys = jax.random.split(base, 6)
    owners = spread_owners(subkeys[0], CAP, BLOCKS)
    per_device = F_DEV // BLK
    row_device = jnp.clip(owners + jax.random.randint(subkeys[1], (BLOCKS,), -2, 3), 0, N_FAC - 1)
    col_device = jnp.clip(owners + jax.random.randint(subkeys[2], (BLOCKS,), -2, 3), 0, N_FAC - 1)
    row_block = row_device * per_device + jax.random.randint(subkeys[3], (BLOCKS,), 0, per_device)
    col_block = col_device * per_device + jax.random.randint(subkeys[4], (BLOCKS,), 0, per_device)
    desk_ids = jax.random.randint(subkeys[5], (BLOCKS,), 0, DESKS)
    listing = jnp.stack([row_block, col_block, desk_ids], axis=1).astype(jnp.int32)
    return (listing, owners)


def draw_block_list(key, part):
    return block_plan(key)[0]


def draw_block_owner(key, part):
    return block_plan(key)[1]


def draw_desk_owner(key, part):
    return spread_owners(jax.random.fold_in(key, 23), DESK_DEV, DESKS)


def plant(result, stream_key, low, high):
    place = [jax.random.randint(jax.random.fold_in(stream_key, axis), (), 0, length) for axis, length in enumerate(result.shape)]
    widest = result.shape.index(max(result.shape))
    beside = place[:widest] + [(place[widest] + 1) % result.shape[widest]] + place[widest + 1:]
    return result.at[tuple(place)].set(low).at[tuple(beside)].set(high)


def levels(key, extent, cuts, smallest, top_value):
    def one(axis_at, blocks):
        steps = jax.random.uniform(jax.random.fold_in(jax.random.fold_in(key, 6), axis_at), (blocks,), jnp.float32, smallest / len(cuts), top_value / len(cuts))
        return jnp.repeat(jnp.exp(steps), extent[axis_at] // blocks).reshape((-1,) + (1,) * (len(extent) - axis_at - 1))

    gain = one(*cuts[0])
    for cut in cuts[1:]:
        gain = gain * one(*cut)
    return gain


def noise(key, extent, deviation, reach, pieces=(), kind=jnp.bfloat16):
    drawn = deviation * jax.random.normal(key, extent, jnp.float32)
    if pieces:
        drawn = drawn * levels(key, extent, pieces, -0.22, 0.18)
    return jnp.clip(drawn, -reach, reach).astype(kind)


def setup_inputs(seed: int = 0) -> dict:
    streams_of = jax.random.split(jax.random.key(seed), 9)
    return {
        "loadings": noise(streams_of[0], (FACTORS, K), K ** -0.5, 0.1875, ((0, 8),)),
        "reduced_shocks": noise(streams_of[1], (K, SCEN), 1.0, 6.0, ((1, 4),)),
        "sensitivity": noise(streams_of[2], (FACTORS, DESKS), FACTORS ** -0.5, 0.0625, ((0, 8),)),
        "cross_gamma": noise(streams_of[3], (N_FAC * CAP, BLK, BLK), (BLK * BLK) ** -0.5, 0.005859375, ((0, 8),)),
        "block_list": draw_block_list(jax.random.fold_in(streams_of[8], 71), 0),
        "block_owner": draw_block_owner(jax.random.fold_in(streams_of[8], 71), 0),
        "desk_owner": draw_desk_owner(jax.random.fold_in(streams_of[8], 71), 0),
        "buckets": plant(jax.random.randint(streams_of[7], (FACTORS,), 0, 5), jax.random.fold_in(streams_of[7], 1), 0, 4).astype(jnp.int32),
    }


horizon_weights = (1.0, 1.0, 2.0, 2.0, 6.0)

def owner_ranks(owners):
    position = jnp.arange(owners.shape[0], dtype=jnp.int32)
    same_owner = owners[:, None] == owners[None, :]
    earlier = position[None, :] < position[:, None]
    return lax.optimization_barrier(jnp.sum((same_owner & earlier).astype(jnp.int32), axis=1)).astype(jnp.int32)

def apply_masks(shocks, bucket_ids):
    horizon = jnp.arange(HORIZONS, dtype=jnp.int32)
    keeps_factor = bucket_ids[:, None] >= horizon[None, :]
    masked = jnp.where(keeps_factor[:, :, None], shocks[:, None, :], jnp.zeros((), jnp.bfloat16))
    return masked.reshape(shocks.shape[0], HORIZONS * shocks.shape[1])

def reference(loadings, reduced_shocks, sensitivity, cross_gamma, block_list, block_owner, desk_owner, buckets):
    shocks = jnp.dot(loadings, reduced_shocks, preferred_element_type=jnp.float32).astype(jnp.bfloat16)
    masked = apply_masks(shocks, buckets)
    total = lax.dot_general(sensitivity, masked, (((0,), (0,)), ((), ())), preferred_element_type=jnp.float32)
    block_slot = (block_owner * CAP + owner_ranks(block_owner)).astype(jnp.int32)
    desk_ids = jnp.arange(DESKS, dtype=jnp.int32)

    def add_block(block_index, running):
        block_entry = block_list[block_index]
        matrix = lax.dynamic_index_in_dim(cross_gamma, block_slot[block_index], 0, keepdims=False).astype(jnp.float32)
        row_part = lax.dynamic_slice_in_dim(masked, (block_entry[0] * BLK).astype(jnp.int32), BLK, 0)
        col_part = lax.dynamic_slice_in_dim(masked, (block_entry[1] * BLK).astype(jnp.int32), BLK, 0).astype(jnp.float32)
        product = jnp.dot(matrix, col_part, precision=lax.Precision.HIGHEST, preferred_element_type=jnp.float32)
        quad_term = 0.5 * lax.optimization_barrier(jnp.sum(row_part.astype(jnp.float32) * product, axis=0))
        return running + jnp.where((desk_ids == block_entry[2])[:, None], quad_term[None, :], jnp.zeros((), jnp.float32))
    total = lax.fori_loop(0, BLOCKS, add_block, total)
    desk_slot = (desk_owner * DESK_DEV + owner_ranks(desk_owner)).astype(jnp.int32)
    placement = (desk_slot[:, None] == jnp.arange(DESK_SLOTS, dtype=jnp.int32)[None, :]).astype(jnp.float32)
    profit = lax.dot_general(placement, total, (((0,), (0,)), ((), ())), precision=lax.Precision.HIGHEST, preferred_element_type=jnp.float32)
    profit = profit.reshape(DESK_SLOTS, HORIZONS, SCEN)
    worst_losses = lax.top_k(-profit, TAIL)[0]
    shortfall = lax.optimization_barrier(jnp.mean(worst_losses, axis=2))
    weights = jnp.array(horizon_weights, jnp.float32)
    adjusted = jnp.sqrt(lax.optimization_barrier(jnp.sum(weights[None, :] * shortfall * shortfall, axis=1)) + 1e-06)
    return (profit, shortfall, adjusted)
```

```python
import functools

import jax
import jax.numpy as jnp
from jax import lax
from jax.experimental import pallas as pl
from jax.experimental.pallas import tpu as pltpu
from jax.sharding import PartitionSpec as P

HORIZONS = 5
CAP = 2
REACH = 2
WINDOW = 2 * REACH + 1
GROUP = 32
GROWS = 8
LIST = 8
MESH = pl.DeviceIdType.MESH
F32 = jnp.float32
BF16 = jnp.bfloat16

horizon_weights = (1.0, 1.0, 2.0, 2.0, 6.0)


def dot_nt(a, b):
    return lax.dot_general(a, b, (((1,), (1,)), ((), ())), preferred_element_type=F32)


def one_hot(condition):
    return jnp.where(condition, 1.0, 0.0).astype(BF16)


def exchange(items, i, j):
    high, low = jnp.maximum(items[i], items[j]), jnp.minimum(items[i], items[j])
    items[i], items[j] = high, low


SORT8 = (
    (0, 1), (2, 3), (4, 5), (6, 7), (0, 2), (1, 3), (4, 6), (5, 7), (1, 2), (5, 6),
    (0, 4), (1, 5), (2, 6), (3, 7), (2, 4), (3, 5), (1, 2), (3, 4), (5, 6),
)


def merge_sorted(first, second):
    items = [jnp.maximum(first[i], second[LIST - 1 - i]) for i in range(LIST)]
    for stride in (4, 2, 1):
        for i in range(LIST):
            if not i & stride:
                exchange(items, i, i + stride)
    return items


def tail_mean(losses, tail):
    items = [losses[8 * i : 8 * i + 8] for i in range(LIST)]
    for i, j in SORT8:
        exchange(items, i, j)
    for shift in (4, 2, 1):
        items = merge_sorted(items, [pltpu.roll(item, shift, 0) for item in items])
    items = merge_sorted(items, [pltpu.roll(item, 64, 1) for item in items])
    others = [pltpu.roll(item, 32, 1) for item in items]
    best = [jnp.maximum(items[i], others[tail - 1 - i]) for i in range(tail)]
    return sum(best[1:], best[0]) * (1.0 / tail)


def kernel(
    n, n_scen, tail, desk_dev,
    blist, bowner, desk_owner, buckets, loadings, reduced, sensitivity, gamma,
    profit_out, short_out, adjusted_out,
    lbuf, rbuf, sbuf, gbuf, win, masked, terms, pair_buf, totals, piece_out, piece_in,
    gam, scen_buf, rt_pad,
    local_sem, win_send, win_recv, pair_sem, piece_send, piece_recv, gam_send, gam_recv,
    scen_send, scen_recv,
):
    me = lax.axis_index("fac")
    sc = lax.axis_index("scen")
    nh = n // 2
    core, chip = lax.rem(me, 2), me // 2
    depth, s_dev = reduced.shape
    f_dev = loadings.shape[0]
    desks = sensitivity.shape[1]
    blocks = bowner.shape[0]
    hs = HORIZONS * s_dev

    local = [
        pltpu.make_async_copy(source, target, local_sem.at[i])
        for i, (source, target) in enumerate(
            ((reduced, rbuf), (loadings, lbuf), (sensitivity, sbuf), (gamma, gbuf))
        )
    ]
    for copy in local:
        copy.start()

    barrier = pltpu.get_barrier_semaphore()
    for step in range(1, n):
        pl.semaphore_signal(
            barrier, inc=1, device_id={"fac": lax.rem(me + step, n)}, device_id_type=MESH
        )
    for step in range(1, n_scen):
        pl.semaphore_signal(
            barrier, inc=1, device_id={"scen": lax.rem(sc + step, n_scen)}, device_id_type=MESH
        )

    owner_row = desk_owner[...]
    owns = one_hot(lax.broadcasted_iota(jnp.int32, (n, desks), 0) == owner_row)
    before = one_hot(
        lax.broadcasted_iota(jnp.int32, (desks, desks), 0)
        < lax.broadcasted_iota(jnp.int32, (desks, desks), 1)
    )
    earlier = jnp.dot(owns, before, preferred_element_type=F32)
    rank_row = jnp.sum(owns.astype(F32) * earlier, axis=0, keepdims=True).astype(jnp.int32)
    slot_row = ((owner_row & 1) * nh + (owner_row >> 1)) * GROUP + rank_row
    my_group = core * nh + chip

    bpad = (blocks + 15) // 16 * 16
    block_ids = lax.broadcasted_iota(jnp.int32, (bpad, 1), 0)

    def read_block(b, carry):
        count, live, rows, cols, owner_col, desk_col = carry
        owner = bowner[b]
        mine = owner == me
        live = tuple(
            jnp.where(mine & (count == k), 1, live[k]) for k in range(CAP)
        )
        rows = tuple(
            jnp.where(mine & (count == k), blist[b, 0], rows[k]) for k in range(CAP)
        )
        cols = tuple(
            jnp.where(mine & (count == k), blist[b, 1], cols[k]) for k in range(CAP)
        )
        owner_col = jnp.where(block_ids == b, owner, owner_col)
        desk_col = jnp.where(block_ids == b, blist[b, 2], desk_col)
        return count + jnp.where(mine, 1, 0), live, rows, cols, owner_col, desk_col

    empty = jnp.full((bpad, 1), -1, jnp.int32)
    zero = jnp.int32(0)
    _, live, rows, cols, owner_col, desk_col = lax.fori_loop(
        0, blocks, read_block, (zero, (zero,) * CAP, (me,) * CAP, (me,) * CAP, empty, empty)
    )
    block_owns = one_hot(owner_col == lax.broadcasted_iota(jnp.int32, (bpad, n), 1))
    above = one_hot(
        lax.broadcasted_iota(jnp.int32, (bpad, bpad), 0)
        > lax.broadcasted_iota(jnp.int32, (bpad, bpad), 1)
    )
    block_earlier = jnp.dot(above, block_owns, preferred_element_type=F32)
    block_rank = jnp.sum(
        block_owns.astype(F32) * block_earlier, axis=1, keepdims=True
    ).astype(jnp.int32)
    distance = me - owner_col
    distance = jnp.where(distance < 0, distance + n, distance)
    key = jnp.where(owner_col >= 0, distance * GROWS + block_rank, -1)
    key_hot = one_hot(key == lax.broadcasted_iota(jnp.int32, (bpad, n * GROWS), 1))
    desk_hot = one_hot(desk_col == lax.broadcasted_iota(jnp.int32, (bpad, desks), 1))
    my_desks = one_hot(
        lax.broadcasted_iota(jnp.int32, (GROUP, desks), 0) + my_group * GROUP == slot_row
    )
    gather_rows = jnp.dot(
        dot_nt(my_desks, desk_hot).astype(BF16), key_hot, preferred_element_type=F32
    )

    local[0].wait()
    rt_pad[...] = jnp.zeros_like(rt_pad)
    rt_pad[0:depth, 0:s_dev] = rbuf[...].astype(F32)
    reduced_t = jnp.transpose(rt_pad[...])[0:s_dev, 0:depth].astype(BF16)
    local[1].wait()
    win[REACH] = dot_nt(reduced_t, lbuf[...]).astype(BF16)

    pl.semaphore_wait(barrier, n - 1 + n_scen - 1)

    def window_copy(step):
        slot = REACH - step
        return pltpu.make_async_remote_copy(
            src_ref=win.at[REACH],
            dst_ref=win.at[slot],
            send_sem=win_send.at[slot],
            recv_sem=win_recv.at[slot],
            device_id={"fac": jnp.clip(me + step, 0, n - 1)},
            device_id_type=MESH,
        )

    steps = [step for step in range(-REACH, REACH + 1) if step]
    for step in steps:
        @pl.when((me + step >= 0) & (me + step < n))
        def _(step=step):
            window_copy(step).start()

    def keeps(index):
        return buckets[index]

    def masks(row, shape_rows):
        return [
            jnp.broadcast_to(jnp.where(row >= h, 1.0, 0.0), (shape_rows, f_dev))
            for h in range(HORIZONS)
        ]

    def fill_masked(shocks, row):
        shocks = shocks.astype(F32)
        for h in range(HORIZONS):
            masked[h * s_dev : (h + 1) * s_dev, :] = jnp.where(row >= h, shocks, 0.0).astype(BF16)

    fill_masked(win[REACH], keeps(me))
    local[2].wait()
    chunk = min(n * GROUP, 256)

    def add_terms(i, carry):
        start = pl.multiple_of(i * chunk, chunk)
        place = one_hot(
            lax.broadcasted_iota(jnp.int32, (chunk, desks), 0) + start == slot_row
        )
        placed = dot_nt(place, sbuf[...]).astype(BF16)
        terms[pl.ds(start, chunk), :] = dot_nt(placed, masked[...])
        return carry

    lax.fori_loop(0, n * GROUP // chunk, add_terms, 0)

    half = nh * GROUP
    pair = pltpu.make_async_remote_copy(
        src_ref=terms.at[pl.ds(pl.multiple_of((1 - core) * half, half), half)],
        dst_ref=pair_buf,
        send_sem=pair_sem.at[0],
        recv_sem=pair_sem.at[1],
        device_id={"fac": me + 1 - 2 * core},
        device_id_type=MESH,
    )
    pair.start()
    pair.wait_recv()
    for j in range(nh):
        start = pl.multiple_of(core * half + j * GROUP, GROUP)
        total = terms[pl.ds(start, GROUP), :] + pair_buf[j * GROUP : (j + 1) * GROUP, :]
        totals[j] = total
        piece_out[j] = total.astype(BF16)
    pieces = []
    for step in range(1, nh):
        target = lax.rem(chip + step, nh)
        copy = pltpu.make_async_remote_copy(
            src_ref=piece_out.at[target],
            dst_ref=piece_in.at[step],
            send_sem=piece_send.at[step],
            recv_sem=piece_recv.at[step],
            device_id={"fac": 2 * target + core},
            device_id_type=MESH,
        )
        copy.start()
        pieces.append(copy)

    for step in steps:
        @pl.when((me - step >= 0) & (me - step < n))
        def _(step=step):
            window_copy(step).wait_recv()
    local[3].wait()
    gam[0] = jnp.zeros((GROWS, hs), F32)
    for k in range(CAP):
        fill_masked(win[jnp.clip(cols[k] - me + REACH, 0, WINDOW - 1)], keeps(cols[k]))
        product = dot_nt(masked[...], gbuf[k])
        row_part = win[jnp.clip(rows[k] - me + REACH, 0, WINDOW - 1)].astype(F32)
        row_bucket = keeps(rows[k])
        folded = []
        for h in range(HORIZONS):
            part = jnp.where(row_bucket >= h, row_part, 0.0) * product[h * s_dev : (h + 1) * s_dev]
            folded.append(sum(part[:, i : i + 128] for i in range(0, f_dev, 128)))
        quad = jnp.sum(jnp.transpose(jnp.concatenate(folded, axis=0)), axis=0, keepdims=True)
        gam[0, k : k + 1, :] = quad * (0.5 * live[k].astype(F32))
    rows_out = []
    for step in range(1, n):
        copy = pltpu.make_async_remote_copy(
            src_ref=gam.at[0],
            dst_ref=gam.at[step],
            send_sem=gam_send.at[step],
            recv_sem=gam_recv.at[step],
            device_id={"fac": lax.rem(me + step, n)},
            device_id_type=MESH,
        )
        copy.start()
        rows_out.append(copy)

    own = totals[chip]
    for step, copy in enumerate(pieces, 1):
        copy.wait_recv()
        own = own + piece_in[step].astype(F32)
    for copy in rows_out:
        copy.wait_recv()
    own = own + jnp.dot(
        gather_rows,
        gam[...].reshape(n * GROWS, hs),
        precision=lax.Precision.HIGHEST,
        preferred_element_type=F32,
    )
    scen_buf[0] = own
    scen_copies = []
    for step in range(1, n_scen):
        copy = pltpu.make_async_remote_copy(
            src_ref=scen_buf.at[0],
            dst_ref=scen_buf.at[step],
            send_sem=scen_send.at[step],
            recv_sem=scen_recv.at[step],
            device_id={"scen": lax.rem(sc + step, n_scen)},
            device_id_type=MESH,
        )
        copy.start()
        scen_copies.append(copy)
    for h in range(HORIZONS):
        profit_out[:, h, :] = own[0:desk_dev, h * s_dev : (h + 1) * s_dev]

    for copy in scen_copies:
        copy.wait_recv()
    losses = -jnp.transpose(scen_buf[...].reshape(n_scen * GROUP, hs))
    weighted = jnp.zeros((8, 128), F32)
    table = jnp.zeros((8, 128), F32)
    sublane = lax.broadcasted_iota(jnp.int32, (8, 128), 0)
    for h in range(HORIZONS):
        mean = tail_mean(losses[h * s_dev : (h + 1) * s_dev], tail)
        weighted = weighted + horizon_weights[h] * mean * mean
        table = jnp.where(sublane == h, mean, table)
    adjusted = jnp.sqrt(weighted + 1e-06)
    adjusted_out[...] = adjusted[0:1, 0:desk_dev]
    short_out[...] = jnp.transpose(table)[0:desk_dev, 0:HORIZONS]

    for step in steps:
        @pl.when((me + step >= 0) & (me + step < n))
        def _(step=step):
            window_copy(step).wait_send()
    pair.wait_send()
    for copy in pieces + rows_out + scen_copies:
        copy.wait_send()


def local_program(
    n, n_scen,
    loadings, reduced_shocks, sensitivity, cross_gamma, block_list, block_owner, desk_owner, buckets,
):
    f_dev, depth = loadings.shape
    s_dev = reduced_shocks.shape[1]
    desks = sensitivity.shape[1]
    desk_dev = (desks + n - 1) // n + 1
    hs = HORIZONS * s_dev
    nh = n // 2
    tail = (s_dev * n_scen * 25 + 999) // 1000
    smem = pl.BlockSpec(memory_space=pltpu.SMEM)
    vmem = pl.BlockSpec(memory_space=pltpu.VMEM)
    anywhere = pl.BlockSpec(memory_space=pl.ANY)
    dma = pltpu.SemaphoreType.DMA
    profit, shortfall, adjusted = pl.pallas_call(
        functools.partial(kernel, n, n_scen, tail, desk_dev),
        out_shape=(
            jax.ShapeDtypeStruct((desk_dev, HORIZONS, s_dev), F32),
            jax.ShapeDtypeStruct((desk_dev, HORIZONS), F32),
            jax.ShapeDtypeStruct((1, desk_dev), F32),
        ),
        in_specs=[smem, smem, vmem, vmem, anywhere, anywhere, anywhere, anywhere],
        out_specs=(vmem, vmem, vmem),
        scratch_shapes=[
            pltpu.VMEM((f_dev, depth), BF16),
            pltpu.VMEM((depth, s_dev), BF16),
            pltpu.VMEM((f_dev, desks), BF16),
            pltpu.VMEM((CAP, f_dev, f_dev), BF16),
            pltpu.VMEM((WINDOW, s_dev, f_dev), BF16),
            pltpu.VMEM((hs, f_dev), BF16),
            pltpu.VMEM((n * GROUP, hs), F32),
            pltpu.VMEM((nh * GROUP, hs), F32),
            pltpu.VMEM((nh, GROUP, hs), F32),
            pltpu.VMEM((nh, GROUP, hs), BF16),
            pltpu.VMEM((nh, GROUP, hs), BF16),
            pltpu.VMEM((n, GROWS, hs), F32),
            pltpu.VMEM((n_scen, GROUP, hs), F32),
            pltpu.VMEM((1024, 128), F32),
            dma((4,)),
            dma((WINDOW,)),
            dma((WINDOW,)),
            dma((2,)),
            dma((nh,)),
            dma((nh,)),
            dma((n,)),
            dma((n,)),
            dma((n_scen,)),
            dma((n_scen,)),
        ],
        compiler_params=pltpu.CompilerParams(
            collective_id=0, has_side_effects=True, vmem_limit_bytes=40 * 1024 * 1024
        ),
        name="expected_shortfall",
    )(
        block_list,
        block_owner,
        desk_owner.reshape(1, desks),
        buckets.reshape(n, 1, f_dev),
        loadings,
        reduced_shocks,
        sensitivity,
        cross_gamma,
    )
    return profit, shortfall, adjusted.reshape(desk_dev)


def solution(mesh):
    return jax.shard_map(
        functools.partial(local_program, mesh.shape["fac"], mesh.shape["scen"]),
        mesh=mesh,
        in_specs=(
            P("fac", None),
            P(None, "scen"),
            P("fac", None),
            P("fac", None, None),
            P(),
            P(),
            P(),
            P(),
        ),
        out_specs=(P("fac", None, "scen"), P("fac", None), P("fac")),
        check_vma=False,
    )
```

```python
import functools

import jax
import jax.numpy as jnp
from jax import lax
from jax.experimental import pallas as pl
from jax.experimental.pallas import tpu as pltpu
from jax.sharding import PartitionSpec as P

HORIZONS = 5
CAP = 2
REACH = 2
WINDOW = 2 * REACH + 1
GROUP = 32
PARTS = 2
LANES = 384
LIST = 8
MESH = pl.DeviceIdType.MESH
F32 = jnp.float32
BF16 = jnp.bfloat16

horizon_weights = (1.0, 1.0, 2.0, 2.0, 6.0)


def dot_nt(a, b):
    return lax.dot_general(a, b, (((1,), (1,)), ((), ())), preferred_element_type=F32)


def one_hot(condition):
    return jnp.where(condition, 1.0, 0.0).astype(BF16)


def exchange(items, i, j):
    high, low = jnp.maximum(items[i], items[j]), jnp.minimum(items[i], items[j])
    items[i], items[j] = high, low


SORT8 = (
    (0, 1), (2, 3), (4, 5), (6, 7), (0, 2), (1, 3), (4, 6), (5, 7), (1, 2), (5, 6),
    (0, 4), (1, 5), (2, 6), (3, 7), (2, 4), (3, 5), (1, 2), (3, 4), (5, 6),
)


def merge_sorted(first, second):
    items = [jnp.maximum(first[i], second[LIST - 1 - i]) for i in range(LIST)]
    for stride in (4, 2, 1):
        for i in range(LIST):
            if not i & stride:
                exchange(items, i, i + stride)
    return items


def sorted_tail(losses):
    items = [losses[8 * i : 8 * i + 8] for i in range(LIST)]
    for i, j in SORT8:
        exchange(items, i, j)
    for shift in (4, 2, 1):
        items = merge_sorted(items, [pltpu.roll(item, shift, 0) for item in items])
    return items


def sort_sublanes(tile, sublane, descending):
    for stride in (4, 2, 1):
        first = (sublane & stride) == 0
        other = jnp.where(first, pltpu.roll(tile, 8 - stride, 0), pltpu.roll(tile, stride, 0))
        takes_high = first if descending else jnp.logical_not(first)
        tile = jnp.where(takes_high, jnp.maximum(tile, other), jnp.minimum(tile, other))
    return tile


def tail_kernel(tail, desk_dev, profit, lists, profit_out, short_out, adjusted_out):
    profit_out[...] = profit[:, 0:desk_dev, :]
    shape = (LIST, lists.shape[2])
    sublane = lax.broadcasted_iota(jnp.int32, shape, 0)
    first = sort_sublanes(jnp.maximum(lists[0, 0:8], lists[1, 8:16]), sublane, True)
    second = sort_sublanes(jnp.maximum(lists[2, 0:8], lists[3, 8:16]), sublane, False)
    best = jnp.maximum(first, pltpu.roll(second, LIST - (LIST - tail), 0))
    mean = jnp.sum(jnp.where(sublane < tail, best, 0.0), axis=0, keepdims=True) * (1.0 / tail)
    total = jnp.zeros((1, desk_dev), F32)
    for h in range(HORIZONS):
        row = mean[:, h * GROUP : h * GROUP + desk_dev]
        short_out[h : h + 1, :] = row
        total = total + horizon_weights[h] * row * row
    adjusted_out[...] = jnp.sqrt(total + 1e-06)


def kernel(
    n, n_scen,
    blist, bowner, desk_owner, buckets, loadings, reduced, sensitivity, gamma,
    profit_out, lists_out,
    lbuf, rbuf, sbuf, gbuf, win, masked, terms, pair_buf, totals, piece_out, piece_in,
    gam, lists,
    local_sem, win_send, win_recv, pair_sem, piece_send, piece_recv, gam_send, gam_recv,
    scen_send, scen_recv,
):
    me = lax.axis_index("fac")
    sc = lax.axis_index("scen")
    nh = n // 2
    core, chip = lax.rem(me, 2), me // 2
    s_dev = reduced.shape[0]
    f_dev = loadings.shape[1]
    desks = sensitivity.shape[0]
    blocks = bowner.shape[0]
    hs = HORIZONS * s_dev
    part = f_dev // PARTS

    def columns(i):
        return pl.ds(i * part, part)

    local = [pltpu.make_async_copy(reduced, rbuf, local_sem.at[0])]
    for i in range(PARTS):
        local.append(
            pltpu.make_async_copy(
                loadings.at[:, columns(i)], lbuf.at[:, columns(i)], local_sem.at[1 + i]
            )
        )
    local.append(pltpu.make_async_copy(sensitivity, sbuf, local_sem.at[1 + PARTS]))
    local.append(pltpu.make_async_copy(gamma, gbuf, local_sem.at[2 + PARTS]))
    for copy in local:
        copy.start()

    barrier = pltpu.get_barrier_semaphore()
    for step in range(1, n):
        pl.semaphore_signal(
            barrier, inc=1, device_id={"fac": lax.rem(me + step, n)}, device_id_type=MESH
        )
    for step in range(1, n_scen):
        pl.semaphore_signal(
            barrier, inc=1, device_id={"scen": lax.rem(sc + step, n_scen)}, device_id_type=MESH
        )

    def window_copy(step, i):
        slot = REACH - step
        return pltpu.make_async_remote_copy(
            src_ref=win.at[REACH, :, columns(i)],
            dst_ref=win.at[slot, :, columns(i)],
            send_sem=win_send.at[slot, i],
            recv_sem=win_recv.at[slot, i],
            device_id={"fac": jnp.clip(me + step, 0, n - 1)},
            device_id_type=MESH,
        )

    steps = [step for step in range(-REACH, REACH + 1) if step]
    local[0].wait()
    for i in range(PARTS):
        local[1 + i].wait()
        win[REACH, :, columns(i)] = jnp.dot(
            rbuf[...], lbuf[:, columns(i)], preferred_element_type=F32
        ).astype(BF16)
        if i == 0:
            pl.semaphore_wait(barrier, n - 1 + n_scen - 1)
        for step in steps:
            @pl.when((me + step >= 0) & (me + step < n))
            def _(step=step, i=i):
                window_copy(step, i).start()

    owner_row = desk_owner[...]
    owns = one_hot(lax.broadcasted_iota(jnp.int32, (n, desks), 0) == owner_row)
    before = one_hot(
        lax.broadcasted_iota(jnp.int32, (desks, desks), 0)
        < lax.broadcasted_iota(jnp.int32, (desks, desks), 1)
    )
    earlier = jnp.dot(owns, before, preferred_element_type=F32)
    rank_row = jnp.sum(owns.astype(F32) * earlier, axis=0, keepdims=True).astype(jnp.int32)
    slot_row = ((owner_row & 1) * nh + (owner_row >> 1)) * GROUP + rank_row
    my_group = core * nh + chip

    def fill_masked(shocks, row):
        shocks = shocks.astype(F32)
        for h in range(HORIZONS):
            masked[h * s_dev : (h + 1) * s_dev, :] = jnp.where(row >= h, shocks, 0.0).astype(BF16)

    fill_masked(win[REACH], buckets[me])
    local[1 + PARTS].wait()
    chunk = min(n * GROUP, 256)

    def add_terms(i, carry):
        start = pl.multiple_of(i * chunk, chunk)
        place = one_hot(
            lax.broadcasted_iota(jnp.int32, (chunk, desks), 0) + start == slot_row
        )
        placed = jnp.dot(place, sbuf[...], preferred_element_type=F32).astype(BF16)
        terms[pl.ds(start, chunk), :] = dot_nt(placed, masked[...])
        return carry

    lax.fori_loop(0, n * GROUP // chunk, add_terms, 0)

    half = nh * GROUP
    pair = pltpu.make_async_remote_copy(
        src_ref=terms.at[pl.ds(pl.multiple_of((1 - core) * half, half), half)],
        dst_ref=pair_buf,
        send_sem=pair_sem.at[0],
        recv_sem=pair_sem.at[1],
        device_id={"fac": me + 1 - 2 * core},
        device_id_type=MESH,
    )
    pair.start()

    bpad = (blocks + 15) // 16 * 16
    block_ids = lax.broadcasted_iota(jnp.int32, (bpad, 1), 0)

    def read_block(b, carry):
        count, live, rows, cols, owner_col, desk_col = carry
        owner = bowner[b]
        mine = owner == me
        live = tuple(jnp.where(mine & (count == k), 1, live[k]) for k in range(CAP))
        rows = tuple(jnp.where(mine & (count == k), blist[0, b], rows[k]) for k in range(CAP))
        cols = tuple(jnp.where(mine & (count == k), blist[1, b], cols[k]) for k in range(CAP))
        owner_col = jnp.where(block_ids == b, owner, owner_col)
        desk_col = jnp.where(block_ids == b, blist[2, b], desk_col)
        return count + jnp.where(mine, 1, 0), live, rows, cols, owner_col, desk_col

    empty = jnp.full((bpad, 1), -1, jnp.int32)
    zero = jnp.int32(0)
    _, live, rows, cols, owner_col, desk_col = lax.fori_loop(
        0, blocks, read_block, (zero, (zero,) * CAP, (me,) * CAP, (me,) * CAP, empty, empty)
    )
    block_owns = one_hot(owner_col == lax.broadcasted_iota(jnp.int32, (bpad, n), 1))
    above = one_hot(
        lax.broadcasted_iota(jnp.int32, (bpad, bpad), 0)
        > lax.broadcasted_iota(jnp.int32, (bpad, bpad), 1)
    )
    block_earlier = jnp.dot(above, block_owns, preferred_element_type=F32)
    block_rank = jnp.sum(
        block_owns.astype(F32) * block_earlier, axis=1, keepdims=True
    ).astype(jnp.int32)
    distance = me - owner_col
    distance = jnp.where(distance < 0, distance + n, distance)
    key = jnp.where(owner_col >= 0, block_rank * n + distance, -1)
    key_hot = one_hot(key == lax.broadcasted_iota(jnp.int32, (bpad, CAP * n), 1))
    desk_hot = one_hot(desk_col == lax.broadcasted_iota(jnp.int32, (bpad, desks), 1))
    my_desks = one_hot(
        lax.broadcasted_iota(jnp.int32, (GROUP, desks), 0) + my_group * GROUP == slot_row
    )
    gather_rows = jnp.dot(
        dot_nt(my_desks, desk_hot).astype(BF16), key_hot, preferred_element_type=F32
    )

    pair.wait_recv()
    for j in range(nh):
        start = pl.multiple_of(core * half + j * GROUP, GROUP)
        total = terms[pl.ds(start, GROUP), :] + pair_buf[j * GROUP : (j + 1) * GROUP, :]
        totals[j] = total
        piece_out[j] = total.astype(BF16)
    pieces = []
    for step in range(1, nh):
        target = lax.rem(chip + step, nh)
        copy = pltpu.make_async_remote_copy(
            src_ref=piece_out.at[target],
            dst_ref=piece_in.at[step],
            send_sem=piece_send.at[step],
            recv_sem=piece_recv.at[step],
            device_id={"fac": 2 * target + core},
            device_id_type=MESH,
        )
        copy.start()
        pieces.append(copy)

    for i in range(PARTS):
        for step in steps:
            @pl.when((me - step >= 0) & (me - step < n))
            def _(step=step, i=i):
                window_copy(step, i).wait_recv()
    local[2 + PARTS].wait()
    for k in range(CAP):
        fill_masked(win[jnp.clip(cols[k] - me + REACH, 0, WINDOW - 1)], buckets[cols[k]])
        row_part = win[jnp.clip(rows[k] - me + REACH, 0, WINDOW - 1)].astype(F32)
        row_bucket = buckets[rows[k]]
        folded = [jnp.zeros((s_dev, 128), F32)] * HORIZONS
        for start in range(0, f_dev, 256):
            product = dot_nt(masked[...], gbuf[k, start : start + 256, :])
            for h in range(HORIZONS):
                for i in (0, 128):
                    at = start + i
                    factor = jnp.where(
                        row_bucket[:, at : at + 128] >= h, row_part[:, at : at + 128], 0.0
                    )
                    folded[h] = folded[h] + factor * product[h * s_dev : (h + 1) * s_dev, i : i + 128]
        quad = jnp.sum(jnp.transpose(jnp.concatenate(folded, axis=0)), axis=0, keepdims=True)
        gam[0, :, k * LANES : k * LANES + hs] = quad * (0.5 * live[k].astype(F32))
    rows_out = []
    for step in range(1, n):
        copy = pltpu.make_async_remote_copy(
            src_ref=gam.at[0],
            dst_ref=gam.at[step],
            send_sem=gam_send.at[step],
            recv_sem=gam_recv.at[step],
            device_id={"fac": lax.rem(me + step, n)},
            device_id_type=MESH,
        )
        copy.start()
        rows_out.append(copy)

    own = totals[chip]
    for step, copy in enumerate(pieces, 1):
        copy.wait_recv()
        own = own + piece_in[step].astype(F32)
    for copy in rows_out:
        copy.wait_recv()
    gamma_rows = jnp.concatenate(
        [gam[q, :, k * LANES : k * LANES + hs] for k in range(CAP) for q in range(n)], axis=0
    )
    own = own + jnp.dot(
        gather_rows, gamma_rows, precision=lax.Precision.HIGHEST, preferred_element_type=F32
    )
    stacked = [own[:, h * s_dev : (h + 1) * s_dev] for h in range(HORIZONS)]
    for h in range(HORIZONS):
        profit_out[h] = stacked[h]
    lanes = lists.shape[2]
    stacked.append(jnp.zeros((lanes - HORIZONS * GROUP, s_dev), F32))
    tall = jnp.concatenate(stacked, axis=0)
    tall = jnp.concatenate([tall, jnp.zeros((lanes, 128 - s_dev), F32)], axis=1)
    items = sorted_tail(-jnp.transpose(tall)[0:s_dev])
    sublane = lax.broadcasted_iota(jnp.int32, (LIST, lanes), 0)
    down, up = items[0], items[LIST - 1]
    for i in range(1, LIST):
        down = jnp.where(sublane == i, items[i], down)
        up = jnp.where(sublane == i, items[LIST - 1 - i], up)
    lists[0, 0:LIST] = down
    lists[0, LIST : 2 * LIST] = up
    scen_copies = []
    for step in range(1, n_scen):
        copy = pltpu.make_async_remote_copy(
            src_ref=lists.at[0],
            dst_ref=lists.at[step],
            send_sem=scen_send.at[step],
            recv_sem=scen_recv.at[step],
            device_id={"scen": lax.rem(sc + step, n_scen)},
            device_id_type=MESH,
        )
        copy.start()
        scen_copies.append(copy)

    for i in range(PARTS):
        for step in steps:
            @pl.when((me + step >= 0) & (me + step < n))
            def _(step=step, i=i):
                window_copy(step, i).wait_send()
    pair.wait_send()
    for copy in pieces + rows_out:
        copy.wait_send()
    for copy in scen_copies:
        copy.wait()
    lists_out[...] = lists[...]


def local_program(
    n, n_scen,
    loadings, reduced_shocks, sensitivity, cross_gamma, block_list, block_owner, desk_owner, buckets,
):
    f_dev, depth = loadings.shape
    s_dev = reduced_shocks.shape[1]
    desks = sensitivity.shape[1]
    desk_dev = (desks + n - 1) // n + 1
    hs = HORIZONS * s_dev
    nh = n // 2
    tail = (s_dev * n_scen * 25 + 999) // 1000
    lanes = (HORIZONS * GROUP + 127) // 128 * 128
    smem = pl.BlockSpec(memory_space=pltpu.SMEM)
    vmem = pl.BlockSpec(memory_space=pltpu.VMEM)
    hbm = pl.BlockSpec(memory_space=pltpu.HBM)
    dma = pltpu.SemaphoreType.DMA
    profit, lists = pl.pallas_call(
        functools.partial(kernel, n, n_scen),
        out_shape=(
            jax.ShapeDtypeStruct((HORIZONS, GROUP, s_dev), F32),
            jax.ShapeDtypeStruct((n_scen, 2 * LIST, lanes), F32),
        ),
        in_specs=[smem, smem, vmem, vmem, hbm, hbm, hbm, hbm],
        out_specs=(vmem, vmem),
        scratch_shapes=[
            pltpu.VMEM((depth, f_dev), BF16),
            pltpu.VMEM((s_dev, depth), BF16),
            pltpu.VMEM((desks, f_dev), BF16),
            pltpu.VMEM((CAP, f_dev, f_dev), BF16),
            pltpu.VMEM((WINDOW, s_dev, f_dev), BF16),
            pltpu.VMEM((hs, f_dev), BF16),
            pltpu.VMEM((n * GROUP, hs), F32),
            pltpu.VMEM((nh * GROUP, hs), F32),
            pltpu.VMEM((nh, GROUP, hs), F32),
            pltpu.VMEM((nh, GROUP, hs), BF16),
            pltpu.VMEM((nh, GROUP, hs), BF16),
            pltpu.VMEM((n, 1, CAP * LANES), F32),
            pltpu.VMEM((n_scen, 2 * LIST, lanes), F32),
            dma((3 + PARTS,)),
            dma((WINDOW, PARTS)),
            dma((WINDOW, PARTS)),
            dma((2,)),
            dma((nh,)),
            dma((nh,)),
            dma((n,)),
            dma((n,)),
            dma((n_scen,)),
            dma((n_scen,)),
        ],
        compiler_params=pltpu.CompilerParams(
            collective_id=0, has_side_effects=True, vmem_limit_bytes=55000 * 1024
        ),
        name="profits",
    )(
        block_list.T,
        block_owner,
        desk_owner.reshape(1, desks),
        buckets.reshape(n, 1, f_dev),
        loadings.T,
        reduced_shocks.T,
        sensitivity.T,
        cross_gamma,
    )
    profit, shortfall, adjusted = pl.pallas_call(
        functools.partial(tail_kernel, tail, desk_dev),
        out_shape=(
            jax.ShapeDtypeStruct((HORIZONS, desk_dev, s_dev), F32),
            jax.ShapeDtypeStruct((HORIZONS, desk_dev), F32),
            jax.ShapeDtypeStruct((1, desk_dev), F32),
        ),
        in_specs=[vmem, vmem],
        out_specs=(vmem, vmem, vmem),
        name="tail_means",
    )(profit, lists)
    return jnp.transpose(profit, (1, 0, 2)), shortfall.T, adjusted.reshape(desk_dev)


def solution(mesh):
    return jax.shard_map(
        functools.partial(local_program, mesh.shape["fac"], mesh.shape["scen"]),
        mesh=mesh,
        in_specs=(
            P("fac", None),
            P(None, "scen"),
            P("fac", None),
            P("fac", None, None),
            P(),
            P(),
            P(),
            P(),
        ),
        out_specs=(P("fac", None, "scen"), P("fac", None), P("fac")),
        check_vma=False,
    )
```

```python
import functools

import jax
import jax.numpy as jnp
from jax import lax
from jax.experimental import pallas as pl
from jax.experimental.pallas import tpu as pltpu
from jax.sharding import PartitionSpec as P

HORIZONS = 5
CAP = 2
REACH = 2
WINDOW = 2 * REACH + 1
GROUP = 32
PARTS = 2
LANES = 384
GRANT = 63 * 1024 * 1024
LIST = 8
MESH = pl.DeviceIdType.MESH
F32 = jnp.float32
BF16 = jnp.bfloat16

horizon_weights = (1.0, 1.0, 2.0, 2.0, 6.0)


def dot_nt(a, b):
    return lax.dot_general(a, b, (((1,), (1,)), ((), ())), preferred_element_type=F32)


def one_hot(condition):
    return jnp.where(condition, 1.0, 0.0).astype(BF16)


def exchange(items, i, j):
    high, low = jnp.maximum(items[i], items[j]), jnp.minimum(items[i], items[j])
    items[i], items[j] = high, low


SORT8 = (
    (0, 1), (2, 3), (4, 5), (6, 7), (0, 2), (1, 3), (4, 6), (5, 7), (1, 2), (5, 6),
    (0, 4), (1, 5), (2, 6), (3, 7), (2, 4), (3, 5), (1, 2), (3, 4), (5, 6),
)


def merge_sorted(first, second):
    items = [jnp.maximum(first[i], second[LIST - 1 - i]) for i in range(LIST)]
    for stride in (4, 2, 1):
        for i in range(LIST):
            if not i & stride:
                exchange(items, i, i + stride)
    return items


def sorted_tail(losses):
    items = [losses[8 * i : 8 * i + 8] for i in range(LIST)]
    for i, j in SORT8:
        exchange(items, i, j)
    for shift in (4, 2, 1):
        items = merge_sorted(items, [pltpu.roll(item, shift, 0) for item in items])
    return items


def sort_sublanes(tile, sublane, descending):
    for stride in (4, 2, 1):
        first = (sublane & stride) == 0
        other = jnp.where(first, pltpu.roll(tile, 8 - stride, 0), pltpu.roll(tile, stride, 0))
        takes_high = first if descending else jnp.logical_not(first)
        tile = jnp.where(takes_high, jnp.maximum(tile, other), jnp.minimum(tile, other))
    return tile


def write_kernel(profit, short, adjusted, profit_out, short_out, adjusted_out, sem):
    copies = [
        pltpu.make_async_copy(source, target, sem.at[i])
        for i, (source, target) in enumerate(
            ((profit, profit_out), (short, short_out), (adjusted, adjusted_out))
        )
    ]
    for copy in copies:
        copy.start()
    for copy in copies:
        copy.wait()


def kernel(
    n, n_scen, tail, desk_dev,
    blist_in, bowner_in, desk_owner_in, buckets_in, loadings, reduced, sensitivity, gamma,
    profit_hbm, short_hbm, adjusted_hbm,
    profit_out, short_out, adjusted_out, out_sem,
    blist, bowner, desk_owner, buckets, lbuf, rbuf, sbuf, gbuf, win, masked, terms, pair_buf, totals, piece_out, piece_in,
    gam, lists,
    local_sem, win_send, win_recv, pair_sem, piece_send, piece_recv, gam_send, gam_recv,
    scen_send, scen_recv,
):
    me = lax.axis_index("fac")
    sc = lax.axis_index("scen")
    nh = n // 2
    core, chip = lax.rem(me, 2), me // 2
    s_dev = reduced.shape[0]
    f_dev = loadings.shape[1]
    desks = sensitivity.shape[0]
    blocks = bowner_in.shape[0]
    hs = HORIZONS * s_dev
    part = f_dev // PARTS

    def columns(i):
        return pl.ds(i * part, part)

    local = [pltpu.make_async_copy(reduced, rbuf, local_sem.at[0])]
    for i in range(PARTS):
        local.append(
            pltpu.make_async_copy(
                loadings.at[:, columns(i)], lbuf.at[:, columns(i)], local_sem.at[1 + i]
            )
        )
    local.append(pltpu.make_async_copy(sensitivity, sbuf, local_sem.at[1 + PARTS]))
    local.append(pltpu.make_async_copy(gamma, gbuf, local_sem.at[2 + PARTS]))
    small = [
        pltpu.make_async_copy(source, target, local_sem.at[3 + PARTS + i])
        for i, (source, target) in enumerate(
            (
                (desk_owner_in, desk_owner), (buckets_in, buckets),
                (blist_in, blist), (bowner_in, bowner),
            )
        )
    ]
    for copy in local[: 1 + PARTS] + small + local[1 + PARTS :]:
        copy.start()

    barrier = pltpu.get_barrier_semaphore()
    for step in range(1, n):
        pl.semaphore_signal(
            barrier, inc=1, device_id={"fac": lax.rem(me + step, n)}, device_id_type=MESH
        )
    for step in range(1, n_scen):
        pl.semaphore_signal(
            barrier, inc=1, device_id={"scen": lax.rem(sc + step, n_scen)}, device_id_type=MESH
        )

    partner = me + 1 - 2 * core
    side = 2 * core - 1

    def window_copy(index, from_slot, to_slot, i, target):
        return pltpu.make_async_remote_copy(
            src_ref=win.at[from_slot, i],
            dst_ref=win.at[to_slot, i],
            send_sem=win_send.at[index],
            recv_sem=win_recv.at[to_slot, i],
            device_id={"fac": jnp.clip(target, 0, n - 1)},
            device_id_type=MESH,
        )

    has_both = (chip + side >= 0) & (chip + side < nh)
    has_one = (chip - side >= 0) & (chip - side < nh)
    has_left, has_right = chip > 0, chip < nh - 1

    def to_both(i):
        target = 2 * (chip + side) + i
        return window_copy(i, REACH, REACH + me - target, i, target)

    def to_one(i):
        return window_copy(PARTS + i, REACH, REACH + 2 * side, i, me - 2 * side)

    def to_partner(i):
        return window_copy(2 * PARTS + i, REACH, REACH + me - partner, i, partner)

    left_slot, right_slot = REACH - 1 - core, REACH + 2 - core

    def hand_left():
        return window_copy(3 * PARTS, left_slot, left_slot + me - partner, core, partner)

    def hand_right():
        return window_copy(3 * PARTS + 1, right_slot, right_slot + me - partner, core, partner)

    def arrival(slot, i):
        return pltpu.make_async_remote_copy(
            src_ref=win.at[REACH, i],
            dst_ref=win.at[slot, i],
            send_sem=win_send.at[0],
            recv_sem=win_recv.at[slot, i],
            device_id={"fac": partner},
            device_id_type=MESH,
        )

    local[0].wait()
    for i in range(PARTS):
        local[1 + i].wait()
        win[REACH, i] = jnp.dot(
            rbuf[...], lbuf[:, columns(i)], preferred_element_type=F32
        ).astype(BF16)
        if i == 0:
            pl.semaphore_wait(barrier, n - 1 + n_scen - 1)

        @pl.when(has_both)
        def _(i=i):
            to_both(i).start()

        @pl.when(has_one)
        def _(i=i):
            to_one(i).start()

        to_partner(i).start()

    def window(slot):
        return jnp.concatenate([win[slot, i] for i in range(PARTS)], axis=1)

    for copy in small:
        copy.wait()

    owner_row = desk_owner[...]
    owns = one_hot(lax.broadcasted_iota(jnp.int32, (n, desks), 0) == owner_row)
    before = one_hot(
        lax.broadcasted_iota(jnp.int32, (desks, desks), 0)
        < lax.broadcasted_iota(jnp.int32, (desks, desks), 1)
    )
    earlier = jnp.dot(owns, before, preferred_element_type=F32)
    rank_row = jnp.sum(owns.astype(F32) * earlier, axis=0, keepdims=True).astype(jnp.int32)
    slot_row = ((owner_row & 1) * nh + (owner_row >> 1)) * GROUP + rank_row
    my_group = core * nh + chip

    def fill_masked(shocks, row):
        shocks = shocks.astype(F32)
        for h in range(HORIZONS):
            masked[h * s_dev : (h + 1) * s_dev, :] = jnp.where(row >= h, shocks, 0.0).astype(BF16)

    fill_masked(window(REACH), buckets[me])
    local[1 + PARTS].wait()
    chunk = min(n * GROUP, 256)

    def add_terms(i, carry):
        start = pl.multiple_of(i * chunk, chunk)
        place = one_hot(
            lax.broadcasted_iota(jnp.int32, (chunk, desks), 0) + start == slot_row
        )
        placed = jnp.dot(place, sbuf[...], preferred_element_type=F32).astype(BF16)
        terms[pl.ds(start, chunk), :] = dot_nt(placed, masked[...])
        return carry

    lax.fori_loop(0, n * GROUP // chunk, add_terms, 0)

    half = nh * GROUP
    pair = pltpu.make_async_remote_copy(
        src_ref=terms.at[pl.ds(pl.multiple_of((1 - core) * half, half), half)],
        dst_ref=pair_buf,
        send_sem=pair_sem.at[0],
        recv_sem=pair_sem.at[1],
        device_id={"fac": partner},
        device_id_type=MESH,
    )
    pair.start()

    bpad = (blocks + 15) // 16 * 16
    block_ids = lax.broadcasted_iota(jnp.int32, (bpad, 1), 0)

    def read_block(b, carry):
        count, live, rows, cols, owner_col, desk_col = carry
        owner = bowner[b]
        mine = owner == me
        live = tuple(jnp.where(mine & (count == k), 1, live[k]) for k in range(CAP))
        rows = tuple(jnp.where(mine & (count == k), blist[0, b], rows[k]) for k in range(CAP))
        cols = tuple(jnp.where(mine & (count == k), blist[1, b], cols[k]) for k in range(CAP))
        owner_col = jnp.where(block_ids == b, owner, owner_col)
        desk_col = jnp.where(block_ids == b, blist[2, b], desk_col)
        return count + jnp.where(mine, 1, 0), live, rows, cols, owner_col, desk_col

    empty = jnp.full((bpad, 1), -1, jnp.int32)
    zero = jnp.int32(0)
    _, live, rows, cols, owner_col, desk_col = lax.fori_loop(
        0, blocks, read_block, (zero, (zero,) * CAP, (me,) * CAP, (me,) * CAP, empty, empty)
    )
    block_owns = one_hot(owner_col == lax.broadcasted_iota(jnp.int32, (bpad, n), 1))
    above = one_hot(
        lax.broadcasted_iota(jnp.int32, (bpad, bpad), 0)
        > lax.broadcasted_iota(jnp.int32, (bpad, bpad), 1)
    )
    block_earlier = jnp.dot(above, block_owns, preferred_element_type=F32)
    block_rank = jnp.sum(
        block_owns.astype(F32) * block_earlier, axis=1, keepdims=True
    ).astype(jnp.int32)
    distance = me - owner_col
    distance = jnp.where(distance < 0, distance + n, distance)
    key = jnp.where(owner_col >= 0, block_rank * n + distance, -1)
    key_hot = one_hot(key == lax.broadcasted_iota(jnp.int32, (bpad, CAP * n), 1))
    desk_hot = one_hot(desk_col == lax.broadcasted_iota(jnp.int32, (bpad, desks), 1))
    my_desks = one_hot(
        lax.broadcasted_iota(jnp.int32, (GROUP, desks), 0) + my_group * GROUP == slot_row
    )
    gather_rows = jnp.dot(
        dot_nt(my_desks, desk_hot).astype(BF16), key_hot, preferred_element_type=F32
    )

    @pl.when(has_left)
    def _():
        arrival(left_slot, core).wait_recv()
        hand_left().start()

    @pl.when(has_right)
    def _():
        arrival(right_slot, core).wait_recv()
        hand_right().start()

    pair.wait_recv()
    for j in range(nh):
        start = pl.multiple_of(core * half + j * GROUP, GROUP)
        total = terms[pl.ds(start, GROUP), :] + pair_buf[j * GROUP : (j + 1) * GROUP, :]
        totals[j] = total
        piece_out[j] = total.astype(BF16)
    pieces = []
    for step in range(1, nh):
        target = lax.rem(chip + step, nh)
        copy = pltpu.make_async_remote_copy(
            src_ref=piece_out.at[target],
            dst_ref=piece_in.at[step],
            send_sem=piece_send.at[step],
            recv_sem=piece_recv.at[step],
            device_id={"fac": 2 * target + core},
            device_id_type=MESH,
        )
        copy.start()
        pieces.append(copy)

    for i in range(PARTS):
        arrival(REACH + partner - me, i).wait_recv()

        @pl.when(has_both)
        def _(i=i):
            arrival(REACH + 2 * side, i).wait_recv()

    @pl.when(has_left)
    def _():
        arrival(left_slot, 1 - core).wait_recv()

    @pl.when(has_right)
    def _():
        arrival(right_slot, 1 - core).wait_recv()

    local[2 + PARTS].wait()
    for k in range(CAP):
        fill_masked(window(jnp.clip(cols[k] - me + REACH, 0, WINDOW - 1)), buckets[cols[k]])
        row_part = window(jnp.clip(rows[k] - me + REACH, 0, WINDOW - 1)).astype(F32)
        row_bucket = buckets[rows[k]]
        folded = [jnp.zeros((s_dev, 128), F32)] * HORIZONS
        for start in range(0, f_dev, 256):
            product = dot_nt(masked[...], gbuf[k, start : start + 256, :])
            for h in range(HORIZONS):
                for i in (0, 128):
                    at = start + i
                    factor = jnp.where(
                        row_bucket[:, at : at + 128] >= h, row_part[:, at : at + 128], 0.0
                    )
                    folded[h] = folded[h] + factor * product[h * s_dev : (h + 1) * s_dev, i : i + 128]
        quad = jnp.sum(jnp.transpose(jnp.concatenate(folded, axis=0)), axis=0, keepdims=True)
        gam[0, :, k * LANES : k * LANES + hs] = quad * (0.5 * live[k].astype(F32))
    rows_out = []
    for step in range(1, n):
        copy = pltpu.make_async_remote_copy(
            src_ref=gam.at[0],
            dst_ref=gam.at[step],
            send_sem=gam_send.at[step],
            recv_sem=gam_recv.at[step],
            device_id={"fac": lax.rem(me + step, n)},
            device_id_type=MESH,
        )
        copy.start()
        rows_out.append(copy)

    own = totals[chip]
    for step, copy in enumerate(pieces, 1):
        copy.wait_recv()
        own = own + piece_in[step].astype(F32)
    for copy in rows_out:
        copy.wait_recv()
    gamma_rows = jnp.concatenate(
        [gam[q, :, k * LANES : k * LANES + hs] for k in range(CAP) for q in range(n)], axis=0
    )
    own = own + jnp.dot(
        gather_rows, gamma_rows, precision=lax.Precision.HIGHEST, preferred_element_type=F32
    )
    stacked = [own[:, h * s_dev : (h + 1) * s_dev] for h in range(HORIZONS)]
    for h in range(HORIZONS):
        profit_out[h] = stacked[h][0:desk_dev]
    write_profit = pltpu.make_async_copy(profit_out, profit_hbm, out_sem.at[0])
    write_profit.start()
    lanes = lists.shape[2]
    stacked.append(jnp.zeros((lanes - HORIZONS * GROUP, s_dev), F32))
    tall = jnp.concatenate(stacked, axis=0)
    tall = jnp.concatenate([tall, jnp.zeros((lanes, 128 - s_dev), F32)], axis=1)
    items = sorted_tail(-jnp.transpose(tall)[0:s_dev])
    sublane = lax.broadcasted_iota(jnp.int32, (LIST, lanes), 0)
    down, up = items[0], items[LIST - 1]
    for i in range(1, LIST):
        down = jnp.where(sublane == i, items[i], down)
        up = jnp.where(sublane == i, items[LIST - 1 - i], up)
    lists[0, 0:LIST] = down
    lists[0, LIST : 2 * LIST] = up
    scen_copies = []
    for step in range(1, n_scen):
        copy = pltpu.make_async_remote_copy(
            src_ref=lists.at[0],
            dst_ref=lists.at[step],
            send_sem=scen_send.at[step],
            recv_sem=scen_recv.at[step],
            device_id={"scen": lax.rem(sc + step, n_scen)},
            device_id_type=MESH,
        )
        copy.start()
        scen_copies.append(copy)

    for i in range(PARTS):
        @pl.when(has_both)
        def _(i=i):
            to_both(i).wait_send()

        @pl.when(has_one)
        def _(i=i):
            to_one(i).wait_send()

        to_partner(i).wait_send()

    @pl.when(has_left)
    def _():
        hand_left().wait_send()

    @pl.when(has_right)
    def _():
        hand_right().wait_send()

    pair.wait_send()
    for copy in pieces + rows_out:
        copy.wait_send()
    for copy in scen_copies:
        copy.wait()

    first = sort_sublanes(jnp.maximum(lists[0, 0:LIST], lists[1, LIST:]), sublane, True)
    second = sort_sublanes(jnp.maximum(lists[2, 0:LIST], lists[3, LIST:]), sublane, False)
    best = jnp.maximum(first, pltpu.roll(second, tail, 0))
    mean = jnp.sum(jnp.where(sublane < tail, best, 0.0), axis=0, keepdims=True) * (1.0 / tail)
    total = jnp.zeros((1, desk_dev), F32)
    for h in range(HORIZONS):
        row = mean[:, h * GROUP : h * GROUP + desk_dev]
        short_out[h : h + 1, :] = row
        total = total + horizon_weights[h] * row * row
    adjusted_out[...] = jnp.sqrt(total + 1e-06)
    write_short = pltpu.make_async_copy(short_out, short_hbm, out_sem.at[1])
    write_adjusted = pltpu.make_async_copy(adjusted_out, adjusted_hbm, out_sem.at[2])
    write_short.start()
    write_adjusted.start()
    for copy in (write_profit, write_short, write_adjusted):
        copy.wait()


def local_program(
    n, n_scen,
    loadings, reduced_shocks, sensitivity, cross_gamma, block_list, block_owner, desk_owner, buckets,
):
    f_dev, depth = loadings.shape
    s_dev = reduced_shocks.shape[1]
    desks = sensitivity.shape[1]
    desk_dev = (desks + n - 1) // n + 1
    hs = HORIZONS * s_dev
    nh = n // 2
    tail = (s_dev * n_scen * 25 + 999) // 1000
    lanes = (HORIZONS * GROUP + 127) // 128 * 128
    anywhere = pl.BlockSpec(memory_space=pl.ANY)
    dma = pltpu.SemaphoreType.DMA
    outputs = (
        jax.ShapeDtypeStruct((HORIZONS, desk_dev, s_dev), F32),
        jax.ShapeDtypeStruct((HORIZONS, desk_dev), F32),
        jax.ShapeDtypeStruct((1, desk_dev), F32),
    )
    results = pl.pallas_call(
        functools.partial(kernel, n, n_scen, tail, desk_dev),
        out_shape=outputs,
        in_specs=[anywhere] * 8,
        out_specs=(anywhere,) * 3,
        scratch_shapes=[
            pltpu.VMEM((HORIZONS, desk_dev, s_dev), F32),
            pltpu.VMEM((HORIZONS, desk_dev), F32),
            pltpu.VMEM((1, desk_dev), F32),
            dma((3,)),
            pltpu.SMEM((3, block_owner.shape[0]), jnp.int32),
            pltpu.SMEM((block_owner.shape[0],), jnp.int32),
            pltpu.VMEM((1, desks), jnp.int32),
            pltpu.VMEM((n, 1, f_dev), jnp.int32),
            pltpu.VMEM((depth, f_dev), BF16),
            pltpu.VMEM((s_dev, depth), BF16),
            pltpu.VMEM((desks, f_dev), BF16),
            pltpu.VMEM((CAP, f_dev, f_dev), BF16),
            pltpu.VMEM((WINDOW, PARTS, s_dev, f_dev // PARTS), BF16),
            pltpu.VMEM((hs, f_dev), BF16),
            pltpu.VMEM((n * GROUP, hs), F32),
            pltpu.VMEM((nh * GROUP, hs), F32),
            pltpu.VMEM((nh, GROUP, hs), F32),
            pltpu.VMEM((nh, GROUP, hs), BF16),
            pltpu.VMEM((nh, GROUP, hs), BF16),
            pltpu.VMEM((n, 1, CAP * LANES), F32),
            pltpu.VMEM((n_scen, 2 * LIST, lanes), F32),
            dma((7 + PARTS,)),
            dma((3 * PARTS + 2,)),
            dma((WINDOW, PARTS)),
            dma((2,)),
            dma((nh,)),
            dma((nh,)),
            dma((n,)),
            dma((n,)),
            dma((n_scen,)),
            dma((n_scen,)),
        ],
        compiler_params=pltpu.CompilerParams(
            collective_id=0, has_side_effects=True, vmem_limit_bytes=GRANT
        ),
        name="profits",
    )(
        block_list.T,
        block_owner,
        desk_owner.reshape(1, desks),
        buckets.reshape(n, 1, f_dev),
        loadings.T,
        reduced_shocks.T,
        sensitivity.T,
        cross_gamma,
    )
    profit, shortfall, adjusted = pl.pallas_call(
        write_kernel,
        out_shape=outputs,
        in_specs=[anywhere] * 3,
        out_specs=(anywhere,) * 3,
        scratch_shapes=[dma((3,))],
        compiler_params=pltpu.CompilerParams(vmem_limit_bytes=GRANT),
        name="write_results",
    )(*results)
    return jnp.transpose(profit, (1, 0, 2)), shortfall.T, adjusted.reshape(desk_dev)


def solution(mesh):
    return jax.shard_map(
        functools.partial(local_program, mesh.shape["fac"], mesh.shape["scen"]),
        mesh=mesh,
        in_specs=(
            P("fac", None),
            P(None, "scen"),
            P("fac", None),
            P("fac", None, None),
            P(),
            P(),
            P(),
            P(),
        ),
        out_specs=(P("fac", None, "scen"), P("fac", None), P("fac")),
        check_vma=False,
    )
```

```python
import functools

import jax
import jax.numpy as jnp
from jax import lax
from jax.experimental import pallas as pl
from jax.experimental.pallas import tpu as pltpu
from jax.sharding import PartitionSpec as P

HORIZONS = 5
CAP = 2
REACH = 2
WINDOW = 2 * REACH + 1
GROUP = 32
PARTS = 2
LANES = 384
GRANT = 63 * 1024 * 1024
LIST = 8
MESH = pl.DeviceIdType.MESH
F32 = jnp.float32
BF16 = jnp.bfloat16

horizon_weights = (1.0, 1.0, 2.0, 2.0, 6.0)


def dot_nt(a, b):
    return lax.dot_general(a, b, (((1,), (1,)), ((), ())), preferred_element_type=F32)


def one_hot(condition):
    return jnp.where(condition, 1.0, 0.0).astype(BF16)


def exchange(items, i, j):
    high, low = jnp.maximum(items[i], items[j]), jnp.minimum(items[i], items[j])
    items[i], items[j] = high, low


SORT8 = (
    (0, 1), (2, 3), (4, 5), (6, 7), (0, 2), (1, 3), (4, 6), (5, 7), (1, 2), (5, 6),
    (0, 4), (1, 5), (2, 6), (3, 7), (2, 4), (3, 5), (1, 2), (3, 4), (5, 6),
)


def merge_sorted(first, second):
    items = [jnp.maximum(first[i], second[LIST - 1 - i]) for i in range(LIST)]
    for stride in (4, 2, 1):
        for i in range(LIST):
            if not i & stride:
                exchange(items, i, i + stride)
    return items


def sorted_tail(losses):
    items = [losses[8 * i : 8 * i + 8] for i in range(LIST)]
    for i, j in SORT8:
        exchange(items, i, j)
    for shift in (4, 2, 1):
        items = merge_sorted(items, [pltpu.roll(item, shift, 0) for item in items])
    return items


def sort_sublanes(tile, sublane, descending):
    for stride in (4, 2, 1):
        first = (sublane & stride) == 0
        other = jnp.where(first, pltpu.roll(tile, 8 - stride, 0), pltpu.roll(tile, stride, 0))
        takes_high = first if descending else jnp.logical_not(first)
        tile = jnp.where(takes_high, jnp.maximum(tile, other), jnp.minimum(tile, other))
    return tile


def write_kernel(
    profit, short, adjusted, profit_out, short_out, adjusted_out, profit_v, short_v, adjusted_v, sem
):
    held = (profit_v, short_v, adjusted_v)
    first = [
        pltpu.make_async_copy(source, target, sem.at[0, i])
        for i, (source, target) in enumerate(zip((profit, short, adjusted), held))
    ]
    second = [
        pltpu.make_async_copy(source, target, sem.at[1, i])
        for i, (source, target) in enumerate(zip(held, (profit_out, short_out, adjusted_out)))
    ]
    for copy in first:
        copy.start()
    for before, copy in zip(first, second):
        before.wait()
        copy.start()
    for copy in second:
        copy.wait()


def kernel(
    n, n_scen, tail, desk_dev,
    blist_in, bowner_in, desk_owner_in, buckets_in, loadings, reduced, sensitivity, gamma,
    profit_hbm, short_hbm, adjusted_hbm,
    profit_out, short_out, adjusted_out, out_sem,
    blist, bowner, desk_owner, buckets, lbuf, rbuf, sbuf, gbuf, win, masked, terms, pair_buf, totals, piece_out, piece_in,
    gam, lists,
    local_sem, win_send, win_recv, pair_sem, piece_send, piece_recv, gam_send, gam_recv,
    scen_send, scen_recv,
):
    me = lax.axis_index("fac")
    sc = lax.axis_index("scen")
    nh = n // 2
    core, chip = lax.rem(me, 2), me // 2
    s_dev = reduced.shape[0]
    f_dev = loadings.shape[1]
    desks = sensitivity.shape[0]
    blocks = bowner_in.shape[0]
    hs = HORIZONS * s_dev
    part = f_dev // PARTS

    def columns(i):
        return pl.ds(i * part, part)

    local = [pltpu.make_async_copy(reduced, rbuf, local_sem.at[0])]
    for i in range(PARTS):
        local.append(
            pltpu.make_async_copy(
                loadings.at[:, columns(i)], lbuf.at[:, columns(i)], local_sem.at[1 + i]
            )
        )
    local.append(pltpu.make_async_copy(sensitivity, sbuf, local_sem.at[1 + PARTS]))
    local.append(pltpu.make_async_copy(gamma, gbuf, local_sem.at[2 + PARTS]))
    small = [
        pltpu.make_async_copy(source, target, local_sem.at[3 + PARTS + i])
        for i, (source, target) in enumerate(
            (
                (desk_owner_in, desk_owner), (buckets_in, buckets),
                (blist_in, blist), (bowner_in, bowner),
            )
        )
    ]
    for copy in local[: 1 + PARTS] + small + local[1 + PARTS :]:
        copy.start()

    barrier = pltpu.get_barrier_semaphore()
    for step in range(1, n):
        pl.semaphore_signal(
            barrier, inc=1, device_id={"fac": lax.rem(me + step, n)}, device_id_type=MESH
        )
    for step in range(1, n_scen):
        pl.semaphore_signal(
            barrier, inc=1, device_id={"scen": lax.rem(sc + step, n_scen)}, device_id_type=MESH
        )

    partner = me + 1 - 2 * core
    side = 2 * core - 1

    def window_copy(index, from_slot, to_slot, i, target):
        return pltpu.make_async_remote_copy(
            src_ref=win.at[from_slot, i],
            dst_ref=win.at[to_slot, i],
            send_sem=win_send.at[index],
            recv_sem=win_recv.at[to_slot, i],
            device_id={"fac": jnp.clip(target, 0, n - 1)},
            device_id_type=MESH,
        )

    has_both = (chip + side >= 0) & (chip + side < nh)
    has_one = (chip - side >= 0) & (chip - side < nh)
    has_left, has_right = chip > 0, chip < nh - 1

    def to_both(i):
        target = 2 * (chip + side) + i
        return window_copy(i, REACH, REACH + me - target, i, target)

    def to_one(i):
        return window_copy(PARTS + i, REACH, REACH + 2 * side, i, me - 2 * side)

    def to_partner(i):
        return window_copy(2 * PARTS + i, REACH, REACH + me - partner, i, partner)

    left_slot, right_slot = REACH - 1 - core, REACH + 2 - core

    def hand_left():
        return window_copy(3 * PARTS, left_slot, left_slot + me - partner, core, partner)

    def hand_right():
        return window_copy(3 * PARTS + 1, right_slot, right_slot + me - partner, core, partner)

    def arrival(slot, i):
        return pltpu.make_async_remote_copy(
            src_ref=win.at[REACH, i],
            dst_ref=win.at[slot, i],
            send_sem=win_send.at[0],
            recv_sem=win_recv.at[slot, i],
            device_id={"fac": partner},
            device_id_type=MESH,
        )

    local[0].wait()
    for i in range(PARTS):
        local[1 + i].wait()
        win[REACH, i] = jnp.dot(
            rbuf[...], lbuf[:, columns(i)], preferred_element_type=F32
        ).astype(BF16)
        if i == 0:
            pl.semaphore_wait(barrier, n - 1 + n_scen - 1)

        @pl.when(has_both)
        def _(i=i):
            to_both(i).start()

        @pl.when(has_one)
        def _(i=i):
            to_one(i).start()

        to_partner(i).start()

    def window(slot):
        return jnp.concatenate([win[slot, i] for i in range(PARTS)], axis=1)

    for copy in small:
        copy.wait()

    owner_row = desk_owner[...]
    owns = one_hot(lax.broadcasted_iota(jnp.int32, (n, desks), 0) == owner_row)
    before = one_hot(
        lax.broadcasted_iota(jnp.int32, (desks, desks), 0)
        < lax.broadcasted_iota(jnp.int32, (desks, desks), 1)
    )
    earlier = jnp.dot(owns, before, preferred_element_type=F32)
    rank_row = jnp.sum(owns.astype(F32) * earlier, axis=0, keepdims=True).astype(jnp.int32)
    slot_row = ((owner_row & 1) * nh + (owner_row >> 1)) * GROUP + rank_row
    my_group = core * nh + chip

    def fill_masked(shocks, row):
        shocks = shocks.astype(F32)
        for h in range(HORIZONS):
            masked[h * s_dev : (h + 1) * s_dev, :] = jnp.where(row >= h, shocks, 0.0).astype(BF16)

    fill_masked(window(REACH), buckets[me])
    local[1 + PARTS].wait()
    chunk = min(n * GROUP, 256)

    def add_terms(i, carry):
        start = pl.multiple_of(i * chunk, chunk)
        place = one_hot(
            lax.broadcasted_iota(jnp.int32, (chunk, desks), 0) + start == slot_row
        )
        placed = jnp.dot(place, sbuf[...], preferred_element_type=F32).astype(BF16)
        terms[pl.ds(start, chunk), :] = dot_nt(placed, masked[...])
        return carry

    lax.fori_loop(0, n * GROUP // chunk, add_terms, 0)

    half = nh * GROUP
    pair = pltpu.make_async_remote_copy(
        src_ref=terms.at[pl.ds(pl.multiple_of((1 - core) * half, half), half)],
        dst_ref=pair_buf,
        send_sem=pair_sem.at[0],
        recv_sem=pair_sem.at[1],
        device_id={"fac": partner},
        device_id_type=MESH,
    )
    pair.start()

    bpad = (blocks + 15) // 16 * 16
    block_ids = lax.broadcasted_iota(jnp.int32, (bpad, 1), 0)

    def read_block(b, carry):
        count, live, rows, cols, owner_col, desk_col = carry
        owner = bowner[b]
        mine = owner == me
        live = tuple(jnp.where(mine & (count == k), 1, live[k]) for k in range(CAP))
        rows = tuple(jnp.where(mine & (count == k), blist[0, b], rows[k]) for k in range(CAP))
        cols = tuple(jnp.where(mine & (count == k), blist[1, b], cols[k]) for k in range(CAP))
        owner_col = jnp.where(block_ids == b, owner, owner_col)
        desk_col = jnp.where(block_ids == b, blist[2, b], desk_col)
        return count + jnp.where(mine, 1, 0), live, rows, cols, owner_col, desk_col

    empty = jnp.full((bpad, 1), -1, jnp.int32)
    zero = jnp.int32(0)
    _, live, rows, cols, owner_col, desk_col = lax.fori_loop(
        0, blocks, read_block, (zero, (zero,) * CAP, (me,) * CAP, (me,) * CAP, empty, empty)
    )
    block_owns = one_hot(owner_col == lax.broadcasted_iota(jnp.int32, (bpad, n), 1))
    above = one_hot(
        lax.broadcasted_iota(jnp.int32, (bpad, bpad), 0)
        > lax.broadcasted_iota(jnp.int32, (bpad, bpad), 1)
    )
    block_earlier = jnp.dot(above, block_owns, preferred_element_type=F32)
    block_rank = jnp.sum(
        block_owns.astype(F32) * block_earlier, axis=1, keepdims=True
    ).astype(jnp.int32)
    distance = me - owner_col
    distance = jnp.where(distance < 0, distance + n, distance)
    key = jnp.where(owner_col >= 0, block_rank * n + distance, -1)
    key_hot = one_hot(key == lax.broadcasted_iota(jnp.int32, (bpad, CAP * n), 1))
    desk_hot = one_hot(desk_col == lax.broadcasted_iota(jnp.int32, (bpad, desks), 1))
    my_desks = one_hot(
        lax.broadcasted_iota(jnp.int32, (GROUP, desks), 0) + my_group * GROUP == slot_row
    )
    gather_rows = jnp.dot(
        dot_nt(my_desks, desk_hot).astype(BF16), key_hot, preferred_element_type=F32
    )

    pair.wait_recv()
    for j in range(nh):
        start = pl.multiple_of(core * half + j * GROUP, GROUP)
        total = terms[pl.ds(start, GROUP), :] + pair_buf[j * GROUP : (j + 1) * GROUP, :]
        totals[j] = total
        piece_out[j] = total.astype(BF16)
    pieces = []
    for step in range(1, nh):
        target = lax.rem(chip + step, nh)
        copy = pltpu.make_async_remote_copy(
            src_ref=piece_out.at[target],
            dst_ref=piece_in.at[step],
            send_sem=piece_send.at[step],
            recv_sem=piece_recv.at[step],
            device_id={"fac": 2 * target + core},
            device_id_type=MESH,
        )
        copy.start()
        pieces.append(copy)

    @pl.when(has_left)
    def _():
        arrival(left_slot, core).wait_recv()
        hand_left().start()

    @pl.when(has_right)
    def _():
        arrival(right_slot, core).wait_recv()
        hand_right().start()

    for i in range(PARTS):
        arrival(REACH + partner - me, i).wait_recv()

        @pl.when(has_both)
        def _(i=i):
            arrival(REACH + 2 * side, i).wait_recv()

    @pl.when(has_left)
    def _():
        arrival(left_slot, 1 - core).wait_recv()

    @pl.when(has_right)
    def _():
        arrival(right_slot, 1 - core).wait_recv()

    local[2 + PARTS].wait()
    for k in range(CAP):
        fill_masked(window(jnp.clip(cols[k] - me + REACH, 0, WINDOW - 1)), buckets[cols[k]])
        row_part = window(jnp.clip(rows[k] - me + REACH, 0, WINDOW - 1)).astype(F32)
        row_bucket = buckets[rows[k]]
        folded = [jnp.zeros((s_dev, 128), F32)] * HORIZONS
        for start in range(0, f_dev, 256):
            product = dot_nt(masked[...], gbuf[k, start : start + 256, :])
            for h in range(HORIZONS):
                for i in (0, 128):
                    at = start + i
                    factor = jnp.where(
                        row_bucket[:, at : at + 128] >= h, row_part[:, at : at + 128], 0.0
                    )
                    folded[h] = folded[h] + factor * product[h * s_dev : (h + 1) * s_dev, i : i + 128]
        quad = jnp.sum(jnp.transpose(jnp.concatenate(folded, axis=0)), axis=0, keepdims=True)
        gam[0, :, k * LANES : k * LANES + hs] = quad * (0.5 * live[k].astype(F32))
    rows_out = []
    for step in range(1, n):
        copy = pltpu.make_async_remote_copy(
            src_ref=gam.at[0],
            dst_ref=gam.at[step],
            send_sem=gam_send.at[step],
            recv_sem=gam_recv.at[step],
            device_id={"fac": lax.rem(me + step, n)},
            device_id_type=MESH,
        )
        copy.start()
        rows_out.append(copy)

    own = totals[chip]
    for step, copy in enumerate(pieces, 1):
        copy.wait_recv()
        own = own + piece_in[step].astype(F32)
    for copy in rows_out:
        copy.wait_recv()
    gamma_rows = jnp.concatenate(
        [gam[q, :, k * LANES : k * LANES + hs] for k in range(CAP) for q in range(n)], axis=0
    )
    own = own + jnp.dot(
        gather_rows, gamma_rows, precision=lax.Precision.HIGHEST, preferred_element_type=F32
    )
    stacked = [own[:, h * s_dev : (h + 1) * s_dev] for h in range(HORIZONS)]
    for h in range(HORIZONS):
        profit_out[h] = stacked[h][0:desk_dev]
    write_profit = pltpu.make_async_copy(profit_out, profit_hbm, out_sem.at[0])
    write_profit.start()
    lanes = lists.shape[2]
    stacked.append(jnp.zeros((lanes - HORIZONS * GROUP, s_dev), F32))
    tall = jnp.concatenate(stacked, axis=0)
    tall = jnp.concatenate([tall, jnp.zeros((lanes, 128 - s_dev), F32)], axis=1)
    items = sorted_tail(-jnp.transpose(tall)[0:s_dev])
    sublane = lax.broadcasted_iota(jnp.int32, (LIST, lanes), 0)
    down, up = items[0], items[LIST - 1]
    for i in range(1, LIST):
        down = jnp.where(sublane == i, items[i], down)
        up = jnp.where(sublane == i, items[LIST - 1 - i], up)
    lists[0, 0:LIST] = down
    lists[0, LIST : 2 * LIST] = up
    scen_copies = []
    for step in range(1, n_scen):
        copy = pltpu.make_async_remote_copy(
            src_ref=lists.at[0],
            dst_ref=lists.at[step],
            send_sem=scen_send.at[step],
            recv_sem=scen_recv.at[step],
            device_id={"scen": lax.rem(sc + step, n_scen)},
            device_id_type=MESH,
        )
        copy.start()
        scen_copies.append(copy)

    for i in range(PARTS):
        @pl.when(has_both)
        def _(i=i):
            to_both(i).wait_send()

        @pl.when(has_one)
        def _(i=i):
            to_one(i).wait_send()

        to_partner(i).wait_send()

    @pl.when(has_left)
    def _():
        hand_left().wait_send()

    @pl.when(has_right)
    def _():
        hand_right().wait_send()

    pair.wait_send()
    for copy in pieces + rows_out:
        copy.wait_send()
    for copy in scen_copies:
        copy.wait()

    first = sort_sublanes(jnp.maximum(lists[0, 0:LIST], lists[1, LIST:]), sublane, True)
    second = sort_sublanes(jnp.maximum(lists[2, 0:LIST], lists[3, LIST:]), sublane, False)
    best = jnp.maximum(first, pltpu.roll(second, tail, 0))
    mean = jnp.sum(jnp.where(sublane < tail, best, 0.0), axis=0, keepdims=True) * (1.0 / tail)
    total = jnp.zeros((1, desk_dev), F32)
    for h in range(HORIZONS):
        row = mean[:, h * GROUP : h * GROUP + desk_dev]
        short_out[h : h + 1, :] = row
        total = total + horizon_weights[h] * row * row
    adjusted_out[...] = jnp.sqrt(total + 1e-06)
    write_short = pltpu.make_async_copy(short_out, short_hbm, out_sem.at[1])
    write_adjusted = pltpu.make_async_copy(adjusted_out, adjusted_hbm, out_sem.at[2])
    write_short.start()
    write_adjusted.start()
    for copy in (write_profit, write_short, write_adjusted):
        copy.wait()


def local_program(
    n, n_scen,
    loadings, reduced_shocks, sensitivity, cross_gamma, block_list, block_owner, desk_owner, buckets,
):
    f_dev, depth = loadings.shape
    s_dev = reduced_shocks.shape[1]
    desks = sensitivity.shape[1]
    desk_dev = (desks + n - 1) // n + 1
    hs = HORIZONS * s_dev
    nh = n // 2
    tail = (s_dev * n_scen * 25 + 999) // 1000
    lanes = (HORIZONS * GROUP + 127) // 128 * 128
    anywhere = pl.BlockSpec(memory_space=pl.ANY)
    dma = pltpu.SemaphoreType.DMA
    outputs = (
        jax.ShapeDtypeStruct((HORIZONS, desk_dev, s_dev), F32),
        jax.ShapeDtypeStruct((HORIZONS, desk_dev), F32),
        jax.ShapeDtypeStruct((1, desk_dev), F32),
    )
    results = pl.pallas_call(
        functools.partial(kernel, n, n_scen, tail, desk_dev),
        out_shape=outputs,
        in_specs=[anywhere] * 8,
        out_specs=(anywhere,) * 3,
        scratch_shapes=[
            pltpu.VMEM((HORIZONS, desk_dev, s_dev), F32),
            pltpu.VMEM((HORIZONS, desk_dev), F32),
            pltpu.VMEM((1, desk_dev), F32),
            dma((3,)),
            pltpu.SMEM((3, block_owner.shape[0]), jnp.int32),
            pltpu.SMEM((block_owner.shape[0],), jnp.int32),
            pltpu.VMEM((1, desks), jnp.int32),
            pltpu.VMEM((n, 1, f_dev), jnp.int32),
            pltpu.VMEM((depth, f_dev), BF16),
            pltpu.VMEM((s_dev, depth), BF16),
            pltpu.VMEM((desks, f_dev), BF16),
            pltpu.VMEM((CAP, f_dev, f_dev), BF16),
            pltpu.VMEM((WINDOW, PARTS, s_dev, f_dev // PARTS), BF16),
            pltpu.VMEM((hs, f_dev), BF16),
            pltpu.VMEM((n * GROUP, hs), F32),
            pltpu.VMEM((nh * GROUP, hs), F32),
            pltpu.VMEM((nh, GROUP, hs), F32),
            pltpu.VMEM((nh, GROUP, hs), BF16),
            pltpu.VMEM((nh, GROUP, hs), BF16),
            pltpu.VMEM((n, 1, CAP * LANES), F32),
            pltpu.VMEM((n_scen, 2 * LIST, lanes), F32),
            dma((7 + PARTS,)),
            dma((3 * PARTS + 2,)),
            dma((WINDOW, PARTS)),
            dma((2,)),
            dma((nh,)),
            dma((nh,)),
            dma((n,)),
            dma((n,)),
            dma((n_scen,)),
            dma((n_scen,)),
        ],
        compiler_params=pltpu.CompilerParams(
            collective_id=0, has_side_effects=True, vmem_limit_bytes=GRANT
        ),
        name="profits",
    )(
        block_list.T,
        block_owner,
        desk_owner.reshape(1, desks),
        buckets.reshape(n, 1, f_dev),
        loadings.T,
        reduced_shocks.T,
        sensitivity.T,
        cross_gamma,
    )
    profit, shortfall, adjusted = pl.pallas_call(
        write_kernel,
        out_shape=outputs,
        in_specs=[anywhere] * 3,
        out_specs=(anywhere,) * 3,
        scratch_shapes=[pltpu.VMEM(out.shape, F32) for out in outputs] + [dma((2, 3))],
        compiler_params=pltpu.CompilerParams(vmem_limit_bytes=GRANT),
        name="write_results",
    )(*results)
    return jnp.transpose(profit, (1, 0, 2)), shortfall.T, adjusted.reshape(desk_dev)


def solution(mesh):
    return jax.shard_map(
        functools.partial(local_program, mesh.shape["fac"], mesh.shape["scen"]),
        mesh=mesh,
        in_specs=(
            P("fac", None),
            P(None, "scen"),
            P("fac", None),
            P("fac", None, None),
            P(),
            P(),
            P(),
            P(),
        ),
        out_specs=(P("fac", None, "scen"), P("fac", None), P("fac")),
        check_vma=False,
    )
```

```python
import functools

import jax
import jax.numpy as jnp
from jax import lax
from jax.experimental import pallas as pl
from jax.experimental.pallas import tpu as pltpu
from jax.sharding import PartitionSpec as P

HORIZONS = 5
CAP = 2
REACH = 2
WINDOW = 2 * REACH + 1
GROUP = 32
PARTS = 2
LANES = 384
GRANT = 63 * 1024 * 1024
LIST = 8
MESH = pl.DeviceIdType.MESH
F32 = jnp.float32
BF16 = jnp.bfloat16

horizon_weights = (1.0, 1.0, 2.0, 2.0, 6.0)


def dot_nt(a, b):
    return lax.dot_general(a, b, (((1,), (1,)), ((), ())), preferred_element_type=F32)


def one_hot(condition):
    return jnp.where(condition, 1.0, 0.0).astype(BF16)


def exchange(items, i, j):
    high, low = jnp.maximum(items[i], items[j]), jnp.minimum(items[i], items[j])
    items[i], items[j] = high, low


SORT8 = (
    (0, 1), (2, 3), (4, 5), (6, 7), (0, 2), (1, 3), (4, 6), (5, 7), (1, 2), (5, 6),
    (0, 4), (1, 5), (2, 6), (3, 7), (2, 4), (3, 5), (1, 2), (3, 4), (5, 6),
)


def merge_sorted(first, second):
    items = [jnp.maximum(first[i], second[LIST - 1 - i]) for i in range(LIST)]
    for stride in (4, 2, 1):
        for i in range(LIST):
            if not i & stride:
                exchange(items, i, i + stride)
    return items


def sorted_tail(losses):
    items = [losses[8 * i : 8 * i + 8] for i in range(LIST)]
    for i, j in SORT8:
        exchange(items, i, j)
    for shift in (4, 2, 1):
        items = merge_sorted(items, [pltpu.roll(item, shift, 0) for item in items])
    return items


def sort_sublanes(tile, sublane, descending):
    for stride in (4, 2, 1):
        first = (sublane & stride) == 0
        other = jnp.where(first, pltpu.roll(tile, 8 - stride, 0), pltpu.roll(tile, stride, 0))
        takes_high = first if descending else jnp.logical_not(first)
        tile = jnp.where(takes_high, jnp.maximum(tile, other), jnp.minimum(tile, other))
    return tile


def write_kernel(
    tail, desk_dev,
    profit, lists_in, profit_out, short_out, adjusted_out, profit_v, lists, short_v, adjusted_v, sem,
):
    read_lists = pltpu.make_async_copy(lists_in, lists, sem.at[0])
    read_profit = pltpu.make_async_copy(profit, profit_v, sem.at[1])
    read_lists.start()
    read_profit.start()
    read_profit.wait()
    writes = [
        pltpu.make_async_copy(source, target, sem.at[2 + i])
        for i, (source, target) in enumerate(
            ((profit_v, profit_out), (short_v, short_out), (adjusted_v, adjusted_out))
        )
    ]
    writes[0].start()
    read_lists.wait()
    sublane = lax.broadcasted_iota(jnp.int32, (LIST, lists.shape[2]), 0)
    first = sort_sublanes(jnp.maximum(lists[0, 0:LIST], lists[1, LIST:]), sublane, True)
    second = sort_sublanes(jnp.maximum(lists[2, 0:LIST], lists[3, LIST:]), sublane, False)
    best = jnp.maximum(first, pltpu.roll(second, tail, 0))
    mean = jnp.sum(jnp.where(sublane < tail, best, 0.0), axis=0, keepdims=True) * (1.0 / tail)
    total = jnp.zeros((1, desk_dev), F32)
    for h in range(HORIZONS):
        row = mean[:, h * GROUP : h * GROUP + desk_dev]
        short_v[h : h + 1, :] = row
        total = total + horizon_weights[h] * row * row
    adjusted_v[...] = jnp.sqrt(total + 1e-06)
    for copy in writes[1:]:
        copy.start()
    for copy in writes:
        copy.wait()


def kernel(
    n, n_scen, desk_dev,
    blist_in, bowner_in, desk_owner_in, buckets_in, loadings, reduced, sensitivity, gamma,
    profit_hbm, lists_hbm, profit_out, out_sem,
    blist, bowner, desk_owner, buckets, lbuf, rbuf, sbuf, gbuf, win, masked, terms, pair_buf, totals, piece_out, piece_in,
    gam, lists,
    local_sem, win_send, win_recv, pair_sem, piece_send, piece_recv, gam_send, gam_recv,
    scen_send, scen_recv,
):
    me = lax.axis_index("fac")
    sc = lax.axis_index("scen")
    nh = n // 2
    core, chip = lax.rem(me, 2), me // 2
    s_dev = reduced.shape[0]
    f_dev = loadings.shape[1]
    desks = sensitivity.shape[0]
    blocks = bowner_in.shape[0]
    hs = HORIZONS * s_dev
    part = f_dev // PARTS

    def columns(i):
        return pl.ds(i * part, part)

    local = [pltpu.make_async_copy(reduced, rbuf, local_sem.at[0])]
    for i in range(PARTS):
        local.append(
            pltpu.make_async_copy(
                loadings.at[:, columns(i)], lbuf.at[:, columns(i)], local_sem.at[1 + i]
            )
        )
    local.append(pltpu.make_async_copy(sensitivity, sbuf, local_sem.at[1 + PARTS]))
    local.append(pltpu.make_async_copy(gamma, gbuf, local_sem.at[2 + PARTS]))
    small = [
        pltpu.make_async_copy(source, target, local_sem.at[3 + PARTS + i])
        for i, (source, target) in enumerate(
            (
                (desk_owner_in, desk_owner), (buckets_in, buckets),
                (blist_in, blist), (bowner_in, bowner),
            )
        )
    ]
    for copy in local[: 1 + PARTS] + small + local[1 + PARTS :]:
        copy.start()

    barrier = pltpu.get_barrier_semaphore()
    for step in range(1, n):
        pl.semaphore_signal(
            barrier, inc=1, device_id={"fac": lax.rem(me + step, n)}, device_id_type=MESH
        )
    for step in range(1, n_scen):
        pl.semaphore_signal(
            barrier, inc=1, device_id={"scen": lax.rem(sc + step, n_scen)}, device_id_type=MESH
        )

    partner = me + 1 - 2 * core
    side = 2 * core - 1

    def window_copy(index, from_slot, to_slot, i, target):
        return pltpu.make_async_remote_copy(
            src_ref=win.at[from_slot, i],
            dst_ref=win.at[to_slot, i],
            send_sem=win_send.at[index],
            recv_sem=win_recv.at[to_slot, i],
            device_id={"fac": jnp.clip(target, 0, n - 1)},
            device_id_type=MESH,
        )

    has_both = (chip + side >= 0) & (chip + side < nh)
    has_one = (chip - side >= 0) & (chip - side < nh)
    has_left, has_right = chip > 0, chip < nh - 1

    def to_both(i):
        target = 2 * (chip + side) + i
        return window_copy(i, REACH, REACH + me - target, i, target)

    def to_one(i):
        return window_copy(PARTS + i, REACH, REACH + 2 * side, i, me - 2 * side)

    def to_partner(i):
        return window_copy(2 * PARTS + i, REACH, REACH + me - partner, i, partner)

    left_slot, right_slot = REACH - 1 - core, REACH + 2 - core

    def hand_left():
        return window_copy(3 * PARTS, left_slot, left_slot + me - partner, core, partner)

    def hand_right():
        return window_copy(3 * PARTS + 1, right_slot, right_slot + me - partner, core, partner)

    def arrival(slot, i):
        return pltpu.make_async_remote_copy(
            src_ref=win.at[REACH, i],
            dst_ref=win.at[slot, i],
            send_sem=win_send.at[0],
            recv_sem=win_recv.at[slot, i],
            device_id={"fac": partner},
            device_id_type=MESH,
        )

    local[0].wait()
    for i in range(PARTS):
        local[1 + i].wait()
        win[REACH, i] = jnp.dot(
            rbuf[...], lbuf[:, columns(i)], preferred_element_type=F32
        ).astype(BF16)
        if i == 0:
            pl.semaphore_wait(barrier, n - 1 + n_scen - 1)

        @pl.when(has_both)
        def _(i=i):
            to_both(i).start()

        @pl.when(has_one)
        def _(i=i):
            to_one(i).start()

        to_partner(i).start()

    def window(slot):
        return jnp.concatenate([win[slot, i] for i in range(PARTS)], axis=1)

    for copy in small:
        copy.wait()

    owner_row = desk_owner[...]
    owns = one_hot(lax.broadcasted_iota(jnp.int32, (n, desks), 0) == owner_row)
    before = one_hot(
        lax.broadcasted_iota(jnp.int32, (desks, desks), 0)
        < lax.broadcasted_iota(jnp.int32, (desks, desks), 1)
    )
    earlier = jnp.dot(owns, before, preferred_element_type=F32)
    rank_row = jnp.sum(owns.astype(F32) * earlier, axis=0, keepdims=True).astype(jnp.int32)
    slot_row = ((owner_row & 1) * nh + (owner_row >> 1)) * GROUP + rank_row
    my_group = core * nh + chip

    def fill_masked(k, shocks, row):
        for h in range(HORIZONS):
            masked[k, h * s_dev : (h + 1) * s_dev, :] = shocks * one_hot(row >= h)

    fill_masked(CAP, window(REACH), buckets[me])
    local[1 + PARTS].wait()
    chunk = min(n * GROUP, 256)

    def add_terms(i, carry):
        start = pl.multiple_of(i * chunk, chunk)
        place = one_hot(
            lax.broadcasted_iota(jnp.int32, (chunk, desks), 0) + start == slot_row
        )
        placed = jnp.dot(place, sbuf[...], preferred_element_type=F32).astype(BF16)
        terms[pl.ds(start, chunk), :] = dot_nt(placed, masked[CAP])
        return carry

    lax.fori_loop(0, n * GROUP // chunk, add_terms, 0)

    half = nh * GROUP
    pair = pltpu.make_async_remote_copy(
        src_ref=terms.at[pl.ds(pl.multiple_of((1 - core) * half, half), half)],
        dst_ref=pair_buf,
        send_sem=pair_sem.at[0],
        recv_sem=pair_sem.at[1],
        device_id={"fac": partner},
        device_id_type=MESH,
    )
    pair.start()

    bpad = (blocks + 15) // 16 * 16
    block_ids = lax.broadcasted_iota(jnp.int32, (bpad, 1), 0)

    def read_block(b, carry):
        count, live, rows, cols, owner_col, desk_col = carry
        owner = bowner[b]
        mine = owner == me
        live = tuple(jnp.where(mine & (count == k), 1, live[k]) for k in range(CAP))
        rows = tuple(jnp.where(mine & (count == k), blist[0, b], rows[k]) for k in range(CAP))
        cols = tuple(jnp.where(mine & (count == k), blist[1, b], cols[k]) for k in range(CAP))
        owner_col = jnp.where(block_ids == b, owner, owner_col)
        desk_col = jnp.where(block_ids == b, blist[2, b], desk_col)
        return count + jnp.where(mine, 1, 0), live, rows, cols, owner_col, desk_col

    empty = jnp.full((bpad, 1), -1, jnp.int32)
    zero = jnp.int32(0)
    _, live, rows, cols, owner_col, desk_col = lax.fori_loop(
        0, blocks, read_block, (zero, (zero,) * CAP, (me,) * CAP, (me,) * CAP, empty, empty)
    )
    block_owns = one_hot(owner_col == lax.broadcasted_iota(jnp.int32, (bpad, n), 1))
    above = one_hot(
        lax.broadcasted_iota(jnp.int32, (bpad, bpad), 0)
        > lax.broadcasted_iota(jnp.int32, (bpad, bpad), 1)
    )
    block_earlier = jnp.dot(above, block_owns, preferred_element_type=F32)
    block_rank = jnp.sum(
        block_owns.astype(F32) * block_earlier, axis=1, keepdims=True
    ).astype(jnp.int32)
    distance = me - owner_col
    distance = jnp.where(distance < 0, distance + n, distance)
    key = jnp.where(owner_col >= 0, block_rank * n + distance, -1)
    key_hot = one_hot(key == lax.broadcasted_iota(jnp.int32, (bpad, CAP * n), 1))
    desk_hot = one_hot(desk_col == lax.broadcasted_iota(jnp.int32, (bpad, desks), 1))
    my_desks = one_hot(
        lax.broadcasted_iota(jnp.int32, (GROUP, desks), 0) + my_group * GROUP == slot_row
    )
    gather_rows = jnp.dot(
        dot_nt(my_desks, desk_hot).astype(BF16), key_hot, preferred_element_type=F32
    )

    pair.wait_recv()
    for j in range(nh):
        start = pl.multiple_of(core * half + j * GROUP, GROUP)
        total = terms[pl.ds(start, GROUP), :] + pair_buf[j * GROUP : (j + 1) * GROUP, :]
        totals[j] = total
        piece_out[j] = total.astype(BF16)
    pieces = []
    for step in range(1, nh):
        target = lax.rem(chip + step, nh)
        copy = pltpu.make_async_remote_copy(
            src_ref=piece_out.at[target],
            dst_ref=piece_in.at[step],
            send_sem=piece_send.at[step],
            recv_sem=piece_recv.at[step],
            device_id={"fac": 2 * target + core},
            device_id_type=MESH,
        )
        copy.start()
        pieces.append(copy)

    @pl.when(has_left)
    def _():
        arrival(left_slot, core).wait_recv()
        hand_left().start()

    @pl.when(has_right)
    def _():
        arrival(right_slot, core).wait_recv()
        hand_right().start()

    for i in range(PARTS):
        arrival(REACH + partner - me, i).wait_recv()

        @pl.when(has_both)
        def _(i=i):
            arrival(REACH + 2 * side, i).wait_recv()

    @pl.when(has_left)
    def _():
        arrival(left_slot, 1 - core).wait_recv()

    @pl.when(has_right)
    def _():
        arrival(right_slot, 1 - core).wait_recv()

    local[2 + PARTS].wait()
    for k in range(CAP):
        fill_masked(k, window(jnp.clip(cols[k] - me + REACH, 0, WINDOW - 1)), buckets[cols[k]])
    for k in range(CAP):
        row_part = window(jnp.clip(rows[k] - me + REACH, 0, WINDOW - 1)).astype(F32)
        row_bucket = buckets[rows[k]]
        folded = [jnp.zeros((s_dev, 128), F32)] * HORIZONS
        for start in range(0, f_dev, 256):
            product = dot_nt(masked[k], gbuf[k, start : start + 256, :])
            for h in range(HORIZONS):
                for i in (0, 128):
                    at = start + i
                    factor = jnp.where(
                        row_bucket[:, at : at + 128] >= h, row_part[:, at : at + 128], 0.0
                    )
                    folded[h] = folded[h] + factor * product[h * s_dev : (h + 1) * s_dev, i : i + 128]
        quad = jnp.sum(jnp.transpose(jnp.concatenate(folded, axis=0)), axis=0, keepdims=True)
        gam[0, :, k * LANES : k * LANES + hs] = quad * (0.5 * live[k].astype(F32))
    rows_out = []
    for step in range(1, n):
        copy = pltpu.make_async_remote_copy(
            src_ref=gam.at[0],
            dst_ref=gam.at[step],
            send_sem=gam_send.at[step],
            recv_sem=gam_recv.at[step],
            device_id={"fac": lax.rem(me + step, n)},
            device_id_type=MESH,
        )
        copy.start()
        rows_out.append(copy)

    own = totals[chip]
    for step, copy in enumerate(pieces, 1):
        copy.wait_recv()
        own = own + piece_in[step].astype(F32)
    for copy in rows_out:
        copy.wait_recv()
    gamma_rows = jnp.concatenate(
        [gam[q, :, k * LANES : k * LANES + hs] for k in range(CAP) for q in range(n)], axis=0
    )
    own = own + jnp.dot(
        gather_rows, gamma_rows, precision=lax.Precision.HIGHEST, preferred_element_type=F32
    )
    stacked = [own[:, h * s_dev : (h + 1) * s_dev] for h in range(HORIZONS)]
    for h in range(HORIZONS):
        profit_out[h] = stacked[h][0:desk_dev]
    write_profit = pltpu.make_async_copy(profit_out, profit_hbm, out_sem.at[0])
    write_profit.start()
    lanes = lists.shape[1]
    stacked.append(jnp.zeros((lanes - HORIZONS * GROUP, s_dev), F32))
    tall = jnp.concatenate(stacked, axis=0)
    tall = jnp.concatenate([tall, jnp.zeros((lanes, 128 - s_dev), F32)], axis=1)
    items = sorted_tail(-jnp.transpose(tall)[0:s_dev])
    sublane = lax.broadcasted_iota(jnp.int32, (LIST, lanes), 0)
    down, up = items[0], items[LIST - 1]
    for i in range(1, LIST):
        down = jnp.where(sublane == i, items[i], down)
        up = jnp.where(sublane == i, items[LIST - 1 - i], up)
    lists[0:LIST] = down
    lists[LIST : 2 * LIST] = up
    scen_copies = []
    for step in range(1, n_scen):
        copy = pltpu.make_async_remote_copy(
            src_ref=lists,
            dst_ref=lists_hbm.at[step],
            send_sem=scen_send.at[step],
            recv_sem=scen_recv.at[step],
            device_id={"scen": lax.rem(sc + step, n_scen)},
            device_id_type=MESH,
        )
        copy.start()
        scen_copies.append(copy)
    write_lists = pltpu.make_async_copy(lists, lists_hbm.at[0], out_sem.at[1])
    write_lists.start()

    for i in range(PARTS):
        @pl.when(has_both)
        def _(i=i):
            to_both(i).wait_send()

        @pl.when(has_one)
        def _(i=i):
            to_one(i).wait_send()

        to_partner(i).wait_send()

    @pl.when(has_left)
    def _():
        hand_left().wait_send()

    @pl.when(has_right)
    def _():
        hand_right().wait_send()

    pair.wait_send()
    for copy in pieces + rows_out:
        copy.wait_send()
    for copy in scen_copies:
        copy.wait()

    write_profit.wait()
    write_lists.wait()


def local_program(
    n, n_scen,
    loadings, reduced_shocks, sensitivity, cross_gamma, block_list, block_owner, desk_owner, buckets,
):
    f_dev, depth = loadings.shape
    s_dev = reduced_shocks.shape[1]
    desks = sensitivity.shape[1]
    desk_dev = (desks + n - 1) // n + 1
    hs = HORIZONS * s_dev
    nh = n // 2
    tail = (s_dev * n_scen * 25 + 999) // 1000
    lanes = (HORIZONS * GROUP + 127) // 128 * 128
    anywhere = pl.BlockSpec(memory_space=pl.ANY)
    dma = pltpu.SemaphoreType.DMA
    outputs = (
        jax.ShapeDtypeStruct((HORIZONS, desk_dev, s_dev), F32),
        jax.ShapeDtypeStruct((HORIZONS, desk_dev), F32),
        jax.ShapeDtypeStruct((1, desk_dev), F32),
    )
    results = pl.pallas_call(
        functools.partial(kernel, n, n_scen, desk_dev),
        out_shape=(outputs[0], jax.ShapeDtypeStruct((n_scen, 2 * LIST, lanes), F32)),
        in_specs=[anywhere] * 8,
        out_specs=(anywhere,) * 2,
        scratch_shapes=[
            pltpu.VMEM((HORIZONS, desk_dev, s_dev), F32),
            dma((2,)),
            pltpu.SMEM((3, block_owner.shape[0]), jnp.int32),
            pltpu.SMEM((block_owner.shape[0],), jnp.int32),
            pltpu.VMEM((1, desks), jnp.int32),
            pltpu.VMEM((n, 1, f_dev), jnp.int32),
            pltpu.VMEM((depth, f_dev), BF16),
            pltpu.VMEM((s_dev, depth), BF16),
            pltpu.VMEM((desks, f_dev), BF16),
            pltpu.VMEM((CAP, f_dev, f_dev), BF16),
            pltpu.VMEM((WINDOW, PARTS, s_dev, f_dev // PARTS), BF16),
            pltpu.VMEM((CAP + 1, hs, f_dev), BF16),
            pltpu.VMEM((n * GROUP, hs), F32),
            pltpu.VMEM((nh * GROUP, hs), F32),
            pltpu.VMEM((nh, GROUP, hs), F32),
            pltpu.VMEM((nh, GROUP, hs), BF16),
            pltpu.VMEM((nh, GROUP, hs), BF16),
            pltpu.VMEM((n, 1, CAP * LANES), F32),
            pltpu.VMEM((2 * LIST, lanes), F32),
            dma((7 + PARTS,)),
            dma((3 * PARTS + 2,)),
            dma((WINDOW, PARTS)),
            dma((2,)),
            dma((nh,)),
            dma((nh,)),
            dma((n,)),
            dma((n,)),
            dma((n_scen,)),
            dma((n_scen,)),
        ],
        compiler_params=pltpu.CompilerParams(
            collective_id=0, has_side_effects=True, vmem_limit_bytes=GRANT
        ),
        name="profits",
    )(
        block_list.T,
        block_owner,
        desk_owner.reshape(1, desks),
        buckets.reshape(n, 1, f_dev),
        loadings.T,
        reduced_shocks.T,
        sensitivity.T,
        cross_gamma,
    )
    profit, shortfall, adjusted = pl.pallas_call(
        functools.partial(write_kernel, tail, desk_dev),
        out_shape=outputs,
        in_specs=[anywhere] * 2,
        out_specs=(anywhere,) * 3,
        scratch_shapes=[
            pltpu.VMEM(outputs[0].shape, F32),
            pltpu.VMEM((n_scen, 2 * LIST, lanes), F32),
            pltpu.VMEM(outputs[1].shape, F32),
            pltpu.VMEM(outputs[2].shape, F32),
            dma((5,)),
        ],
        compiler_params=pltpu.CompilerParams(vmem_limit_bytes=GRANT),
        name="write_results",
    )(*results)
    return jnp.transpose(profit, (1, 0, 2)), shortfall.T, adjusted.reshape(desk_dev)


def solution(mesh):
    return jax.shard_map(
        functools.partial(local_program, mesh.shape["fac"], mesh.shape["scen"]),
        mesh=mesh,
        in_specs=(
            P("fac", None),
            P(None, "scen"),
            P("fac", None),
            P("fac", None, None),
            P(),
            P(),
            P(),
            P(),
        ),
        out_specs=(P("fac", None, "scen"), P("fac", None), P("fac")),
        check_vma=False,
    )
```

```python
import functools

import jax
import jax.numpy as jnp
from jax import lax
from jax.experimental import pallas as pl
from jax.experimental.pallas import tpu as pltpu
from jax.sharding import PartitionSpec as P

HORIZONS = 5
CAP = 2
REACH = 2
WINDOW = 2 * REACH + 1
GROUP = 32
PARTS = 2
LANES = 384
GRANT = 63 * 1024 * 1024
LIST = 8
MESH = pl.DeviceIdType.MESH
F32 = jnp.float32
BF16 = jnp.bfloat16

horizon_weights = (1.0, 1.0, 2.0, 2.0, 6.0)


def dot_nt(a, b):
    return lax.dot_general(a, b, (((1,), (1,)), ((), ())), preferred_element_type=F32)


def one_hot(condition):
    return jnp.where(condition, 1.0, 0.0).astype(BF16)


def exchange(items, i, j):
    high, low = jnp.maximum(items[i], items[j]), jnp.minimum(items[i], items[j])
    items[i], items[j] = high, low


SORT8 = (
    (0, 1), (2, 3), (4, 5), (6, 7), (0, 2), (1, 3), (4, 6), (5, 7), (1, 2), (5, 6),
    (0, 4), (1, 5), (2, 6), (3, 7), (2, 4), (3, 5), (1, 2), (3, 4), (5, 6),
)


def merge_sorted(first, second):
    items = [jnp.maximum(first[i], second[LIST - 1 - i]) for i in range(LIST)]
    for stride in (4, 2, 1):
        for i in range(LIST):
            if not i & stride:
                exchange(items, i, i + stride)
    return items


def sorted_tail(losses):
    items = [losses[8 * i : 8 * i + 8] for i in range(LIST)]
    for i, j in SORT8:
        exchange(items, i, j)
    for shift in (4, 2, 1):
        items = merge_sorted(items, [pltpu.roll(item, shift, 0) for item in items])
    return items


def sort_sublanes(tile, sublane, descending):
    for stride in (4, 2, 1):
        first = (sublane & stride) == 0
        other = jnp.where(first, pltpu.roll(tile, 8 - stride, 0), pltpu.roll(tile, stride, 0))
        takes_high = first if descending else jnp.logical_not(first)
        tile = jnp.where(takes_high, jnp.maximum(tile, other), jnp.minimum(tile, other))
    return tile


def write_kernel(
    tail, desk_dev,
    profit, lists_in, profit_out, short_out, adjusted_out, profit_v, lists, short_v, adjusted_v, sem,
):
    read_lists = pltpu.make_async_copy(lists_in, lists, sem.at[0])
    read_profit = pltpu.make_async_copy(profit, profit_v, sem.at[1])
    read_lists.start()
    read_profit.start()
    read_profit.wait()
    writes = [
        pltpu.make_async_copy(source, target, sem.at[2 + i])
        for i, (source, target) in enumerate(
            ((profit_v, profit_out), (short_v, short_out), (adjusted_v, adjusted_out))
        )
    ]
    writes[0].start()
    read_lists.wait()
    sublane = lax.broadcasted_iota(jnp.int32, (LIST, lists.shape[2]), 0)
    first = sort_sublanes(jnp.maximum(lists[0, 0:LIST], lists[1, LIST:]), sublane, True)
    second = sort_sublanes(jnp.maximum(lists[2, 0:LIST], lists[3, LIST:]), sublane, False)
    best = jnp.maximum(first, pltpu.roll(second, tail, 0))
    mean = jnp.sum(jnp.where(sublane < tail, best, 0.0), axis=0, keepdims=True) * (1.0 / tail)
    total = jnp.zeros((1, desk_dev), F32)
    for h in range(HORIZONS):
        row = mean[:, h * GROUP : h * GROUP + desk_dev]
        short_v[h : h + 1, :] = row
        total = total + horizon_weights[h] * row * row
    adjusted_v[...] = jnp.sqrt(total + 1e-06)
    for copy in writes[1:]:
        copy.start()
    for copy in writes:
        copy.wait()


def kernel(
    n, n_scen, desk_dev,
    blist_in, bowner_in, desk_owner_in, buckets_in, loadings, reduced, sensitivity, gamma,
    profit_hbm, lists_hbm, profit_out, out_sem,
    blist, bowner, desk_owner, buckets, lbuf, rbuf, sbuf, gbuf, win, masked, terms, pair_buf, totals, piece_out, piece_in,
    gam, lists,
    local_sem, win_send, win_recv, pair_sem, piece_send, piece_recv, gam_send, gam_recv,
    scen_send, scen_recv,
):
    me = lax.axis_index("fac")
    sc = lax.axis_index("scen")
    nh = n // 2
    core, chip = lax.rem(me, 2), me // 2
    s_dev = reduced.shape[0]
    f_dev = loadings.shape[1]
    desks = sensitivity.shape[0]
    blocks = bowner_in.shape[0]
    hs = HORIZONS * s_dev
    part = f_dev // PARTS

    def columns(i):
        return pl.ds(i * part, part)

    local = [pltpu.make_async_copy(reduced, rbuf, local_sem.at[0])]
    for i in range(PARTS):
        local.append(
            pltpu.make_async_copy(
                loadings.at[:, columns(i)], lbuf.at[:, columns(i)], local_sem.at[1 + i]
            )
        )
    local.append(pltpu.make_async_copy(sensitivity, sbuf, local_sem.at[1 + PARTS]))
    local.append(pltpu.make_async_copy(gamma, gbuf, local_sem.at[2 + PARTS]))
    small = [
        pltpu.make_async_copy(source, target, local_sem.at[3 + PARTS + i])
        for i, (source, target) in enumerate(
            (
                (desk_owner_in, desk_owner), (buckets_in, buckets),
                (blist_in, blist), (bowner_in, bowner),
            )
        )
    ]
    for copy in local[: 1 + PARTS] + small + local[1 + PARTS :]:
        copy.start()

    barrier = pltpu.get_barrier_semaphore()
    for step in range(1, n):
        pl.semaphore_signal(
            barrier, inc=1, device_id={"fac": lax.rem(me + step, n)}, device_id_type=MESH
        )
    for step in range(1, n_scen):
        pl.semaphore_signal(
            barrier, inc=1, device_id={"scen": lax.rem(sc + step, n_scen)}, device_id_type=MESH
        )

    partner = me + 1 - 2 * core
    side = 2 * core - 1

    def window_copy(index, from_slot, to_slot, i, target):
        return pltpu.make_async_remote_copy(
            src_ref=win.at[from_slot, i],
            dst_ref=win.at[to_slot, i],
            send_sem=win_send.at[index],
            recv_sem=win_recv.at[to_slot, i],
            device_id={"fac": jnp.clip(target, 0, n - 1)},
            device_id_type=MESH,
        )

    has_both = (chip + side >= 0) & (chip + side < nh)
    has_one = (chip - side >= 0) & (chip - side < nh)
    has_left, has_right = chip > 0, chip < nh - 1

    def to_both(i):
        target = 2 * (chip + side) + i
        return window_copy(i, REACH, REACH + me - target, i, target)

    def to_one(i):
        return window_copy(PARTS + i, REACH, REACH + 2 * side, i, me - 2 * side)

    def to_partner(i):
        return window_copy(2 * PARTS + i, REACH, REACH + me - partner, i, partner)

    left_slot, right_slot = REACH - 1 - core, REACH + 2 - core

    def hand_left():
        return window_copy(3 * PARTS, left_slot, left_slot + me - partner, core, partner)

    def hand_right():
        return window_copy(3 * PARTS + 1, right_slot, right_slot + me - partner, core, partner)

    def arrival(slot, i):
        return pltpu.make_async_remote_copy(
            src_ref=win.at[REACH, i],
            dst_ref=win.at[slot, i],
            send_sem=win_send.at[0],
            recv_sem=win_recv.at[slot, i],
            device_id={"fac": partner},
            device_id_type=MESH,
        )

    local[0].wait()
    for i in range(PARTS):
        local[1 + i].wait()
        win[REACH, i] = jnp.dot(
            rbuf[...], lbuf[:, columns(i)], preferred_element_type=F32
        ).astype(BF16)
        if i == 0:
            pl.semaphore_wait(barrier, n - 1 + n_scen - 1)

        @pl.when(has_both)
        def _(i=i):
            to_both(i).start()

        to_partner(i).start()

    def window(slot):
        return jnp.concatenate([win[slot, i] for i in range(PARTS)], axis=1)

    for copy in small:
        copy.wait()

    owner_row = desk_owner[...]
    owns = one_hot(lax.broadcasted_iota(jnp.int32, (n, desks), 0) == owner_row)
    before = one_hot(
        lax.broadcasted_iota(jnp.int32, (desks, desks), 0)
        < lax.broadcasted_iota(jnp.int32, (desks, desks), 1)
    )
    earlier = jnp.dot(owns, before, preferred_element_type=F32)
    rank_row = jnp.sum(owns.astype(F32) * earlier, axis=0, keepdims=True).astype(jnp.int32)
    slot_row = ((owner_row & 1) * nh + (owner_row >> 1)) * GROUP + rank_row
    my_group = core * nh + chip

    def fill_masked(k, shocks, row):
        for h in range(HORIZONS):
            masked[k, h * s_dev : (h + 1) * s_dev, :] = shocks * one_hot(row >= h)

    fill_masked(CAP, window(REACH), buckets[me])
    local[1 + PARTS].wait()
    chunk = min(n * GROUP, 256)

    def add_terms(i, carry):
        start = pl.multiple_of(i * chunk, chunk)
        place = one_hot(
            lax.broadcasted_iota(jnp.int32, (chunk, desks), 0) + start == slot_row
        )
        placed = jnp.dot(place, sbuf[...], preferred_element_type=F32).astype(BF16)
        terms[pl.ds(start, chunk), :] = dot_nt(placed, masked[CAP])
        return carry

    lax.fori_loop(0, n * GROUP // chunk, add_terms, 0)

    half = nh * GROUP
    pair = pltpu.make_async_remote_copy(
        src_ref=terms.at[pl.ds(pl.multiple_of((1 - core) * half, half), half)],
        dst_ref=pair_buf,
        send_sem=pair_sem.at[0],
        recv_sem=pair_sem.at[1],
        device_id={"fac": partner},
        device_id_type=MESH,
    )
    pair.start()

    @pl.when(has_one)
    def _():
        for i in range(PARTS):
            to_one(i).start()

    bpad = (blocks + 15) // 16 * 16
    block_ids = lax.broadcasted_iota(jnp.int32, (bpad, 1), 0)

    def read_block(b, carry):
        count, live, rows, cols, owner_col, desk_col = carry
        owner = bowner[b]
        mine = owner == me
        live = tuple(jnp.where(mine & (count == k), 1, live[k]) for k in range(CAP))
        rows = tuple(jnp.where(mine & (count == k), blist[0, b], rows[k]) for k in range(CAP))
        cols = tuple(jnp.where(mine & (count == k), blist[1, b], cols[k]) for k in range(CAP))
        owner_col = jnp.where(block_ids == b, owner, owner_col)
        desk_col = jnp.where(block_ids == b, blist[2, b], desk_col)
        return count + jnp.where(mine, 1, 0), live, rows, cols, owner_col, desk_col

    empty = jnp.full((bpad, 1), -1, jnp.int32)
    zero = jnp.int32(0)
    _, live, rows, cols, owner_col, desk_col = lax.fori_loop(
        0, blocks, read_block, (zero, (zero,) * CAP, (me,) * CAP, (me,) * CAP, empty, empty)
    )
    block_owns = one_hot(owner_col == lax.broadcasted_iota(jnp.int32, (bpad, n), 1))
    above = one_hot(
        lax.broadcasted_iota(jnp.int32, (bpad, bpad), 0)
        > lax.broadcasted_iota(jnp.int32, (bpad, bpad), 1)
    )
    block_earlier = jnp.dot(above, block_owns, preferred_element_type=F32)
    block_rank = jnp.sum(
        block_owns.astype(F32) * block_earlier, axis=1, keepdims=True
    ).astype(jnp.int32)
    distance = me - owner_col
    distance = jnp.where(distance < 0, distance + n, distance)
    key = jnp.where(owner_col >= 0, block_rank * n + distance, -1)
    key_hot = one_hot(key == lax.broadcasted_iota(jnp.int32, (bpad, CAP * n), 1))
    desk_hot = one_hot(desk_col == lax.broadcasted_iota(jnp.int32, (bpad, desks), 1))
    my_desks = one_hot(
        lax.broadcasted_iota(jnp.int32, (GROUP, desks), 0) + my_group * GROUP == slot_row
    )
    gather_rows = jnp.dot(
        dot_nt(my_desks, desk_hot).astype(BF16), key_hot, preferred_element_type=F32
    )

    pair.wait_recv()
    for j in range(nh):
        start = pl.multiple_of(core * half + j * GROUP, GROUP)
        total = terms[pl.ds(start, GROUP), :] + pair_buf[j * GROUP : (j + 1) * GROUP, :]
        totals[j] = total
        piece_out[j] = total.astype(BF16)
    pieces = []
    for step in range(1, nh):
        target = lax.rem(chip + step, nh)
        copy = pltpu.make_async_remote_copy(
            src_ref=piece_out.at[target],
            dst_ref=piece_in.at[step],
            send_sem=piece_send.at[step],
            recv_sem=piece_recv.at[step],
            device_id={"fac": 2 * target + core},
            device_id_type=MESH,
        )
        copy.start()
        pieces.append(copy)

    @pl.when(has_left)
    def _():
        arrival(left_slot, core).wait_recv()
        hand_left().start()

    @pl.when(has_right)
    def _():
        arrival(right_slot, core).wait_recv()
        hand_right().start()

    for i in range(PARTS):
        arrival(REACH + partner - me, i).wait_recv()

        @pl.when(has_both)
        def _(i=i):
            arrival(REACH + 2 * side, i).wait_recv()

    @pl.when(has_left)
    def _():
        arrival(left_slot, 1 - core).wait_recv()

    @pl.when(has_right)
    def _():
        arrival(right_slot, 1 - core).wait_recv()

    local[2 + PARTS].wait()
    for k in range(CAP):
        fill_masked(k, window(jnp.clip(cols[k] - me + REACH, 0, WINDOW - 1)), buckets[cols[k]])
    for k in range(CAP):
        row_part = window(jnp.clip(rows[k] - me + REACH, 0, WINDOW - 1)).astype(F32)
        row_bucket = buckets[rows[k]]
        folded = [jnp.zeros((s_dev, 128), F32)] * HORIZONS
        for start in range(0, f_dev, 256):
            product = dot_nt(masked[k], gbuf[k, start : start + 256, :])
            for h in range(HORIZONS):
                for i in (0, 128):
                    at = start + i
                    factor = jnp.where(
                        row_bucket[:, at : at + 128] >= h, row_part[:, at : at + 128], 0.0
                    )
                    folded[h] = folded[h] + factor * product[h * s_dev : (h + 1) * s_dev, i : i + 128]
        quad = jnp.sum(jnp.transpose(jnp.concatenate(folded, axis=0)), axis=0, keepdims=True)
        gam[0, :, k * LANES : k * LANES + hs] = quad * (0.5 * live[k].astype(F32))
    rows_out = []
    for step in range(1, n):
        copy = pltpu.make_async_remote_copy(
            src_ref=gam.at[0],
            dst_ref=gam.at[step],
            send_sem=gam_send.at[step],
            recv_sem=gam_recv.at[step],
            device_id={"fac": lax.rem(me + step, n)},
            device_id_type=MESH,
        )
        copy.start()
        rows_out.append(copy)

    own = totals[chip]
    for step, copy in enumerate(pieces, 1):
        copy.wait_recv()
        own = own + piece_in[step].astype(F32)
    for copy in rows_out:
        copy.wait_recv()
    gamma_rows = jnp.concatenate(
        [gam[q, :, k * LANES : k * LANES + hs] for k in range(CAP) for q in range(n)], axis=0
    )
    own = own + jnp.dot(
        gather_rows, gamma_rows, precision=lax.Precision.HIGHEST, preferred_element_type=F32
    )
    stacked = [own[:, h * s_dev : (h + 1) * s_dev] for h in range(HORIZONS)]
    for h in range(HORIZONS):
        profit_out[h] = stacked[h][0:desk_dev]
    write_profit = pltpu.make_async_copy(profit_out, profit_hbm, out_sem.at[0])
    write_profit.start()
    lanes = lists.shape[1]
    stacked.append(jnp.zeros((lanes - HORIZONS * GROUP, s_dev), F32))
    tall = jnp.concatenate(stacked, axis=0)
    tall = jnp.concatenate([tall, jnp.zeros((lanes, 128 - s_dev), F32)], axis=1)
    items = sorted_tail(-jnp.transpose(tall)[0:s_dev])
    sublane = lax.broadcasted_iota(jnp.int32, (LIST, lanes), 0)
    down, up = items[0], items[LIST - 1]
    for i in range(1, LIST):
        down = jnp.where(sublane == i, items[i], down)
        up = jnp.where(sublane == i, items[LIST - 1 - i], up)
    lists[0:LIST] = down
    lists[LIST : 2 * LIST] = up
    scen_copies = []
    for step in range(1, n_scen):
        copy = pltpu.make_async_remote_copy(
            src_ref=lists,
            dst_ref=lists_hbm.at[step],
            send_sem=scen_send.at[step],
            recv_sem=scen_recv.at[step],
            device_id={"scen": lax.rem(sc + step, n_scen)},
            device_id_type=MESH,
        )
        copy.start()
        scen_copies.append(copy)
    write_lists = pltpu.make_async_copy(lists, lists_hbm.at[0], out_sem.at[1])
    write_lists.start()

    for i in range(PARTS):
        @pl.when(has_both)
        def _(i=i):
            to_both(i).wait_send()

        @pl.when(has_one)
        def _(i=i):
            to_one(i).wait_send()

        to_partner(i).wait_send()

    @pl.when(has_left)
    def _():
        hand_left().wait_send()

    @pl.when(has_right)
    def _():
        hand_right().wait_send()

    pair.wait_send()
    for copy in pieces + rows_out:
        copy.wait_send()
    for copy in scen_copies:
        copy.wait()

    write_profit.wait()
    write_lists.wait()


def local_program(
    n, n_scen,
    loadings, reduced_shocks, sensitivity, cross_gamma, block_list, block_owner, desk_owner, buckets,
):
    f_dev, depth = loadings.shape
    s_dev = reduced_shocks.shape[1]
    desks = sensitivity.shape[1]
    desk_dev = (desks + n - 1) // n + 1
    hs = HORIZONS * s_dev
    nh = n // 2
    tail = (s_dev * n_scen * 25 + 999) // 1000
    lanes = (HORIZONS * GROUP + 127) // 128 * 128
    anywhere = pl.BlockSpec(memory_space=pl.ANY)
    dma = pltpu.SemaphoreType.DMA
    outputs = (
        jax.ShapeDtypeStruct((HORIZONS, desk_dev, s_dev), F32),
        jax.ShapeDtypeStruct((HORIZONS, desk_dev), F32),
        jax.ShapeDtypeStruct((1, desk_dev), F32),
    )
    results = pl.pallas_call(
        functools.partial(kernel, n, n_scen, desk_dev),
        out_shape=(outputs[0], jax.ShapeDtypeStruct((n_scen, 2 * LIST, lanes), F32)),
        in_specs=[anywhere] * 8,
        out_specs=(anywhere,) * 2,
        scratch_shapes=[
            pltpu.VMEM((HORIZONS, desk_dev, s_dev), F32),
            dma((2,)),
            pltpu.SMEM((3, block_owner.shape[0]), jnp.int32),
            pltpu.SMEM((block_owner.shape[0],), jnp.int32),
            pltpu.VMEM((1, desks), jnp.int32),
            pltpu.VMEM((n, 1, f_dev), jnp.int32),
            pltpu.VMEM((depth, f_dev), BF16),
            pltpu.VMEM((s_dev, depth), BF16),
            pltpu.VMEM((desks, f_dev), BF16),
            pltpu.VMEM((CAP, f_dev, f_dev), BF16),
            pltpu.VMEM((WINDOW, PARTS, s_dev, f_dev // PARTS), BF16),
            pltpu.VMEM((CAP + 1, hs, f_dev), BF16),
            pltpu.VMEM((n * GROUP, hs), F32),
            pltpu.VMEM((nh * GROUP, hs), F32),
            pltpu.VMEM((nh, GROUP, hs), F32),
            pltpu.VMEM((nh, GROUP, hs), BF16),
            pltpu.VMEM((nh, GROUP, hs), BF16),
            pltpu.VMEM((n, 1, CAP * LANES), F32),
            pltpu.VMEM((2 * LIST, lanes), F32),
            dma((7 + PARTS,)),
            dma((3 * PARTS + 2,)),
            dma((WINDOW, PARTS)),
            dma((2,)),
            dma((nh,)),
            dma((nh,)),
            dma((n,)),
            dma((n,)),
            dma((n_scen,)),
            dma((n_scen,)),
        ],
        compiler_params=pltpu.CompilerParams(
            collective_id=0, has_side_effects=True, vmem_limit_bytes=GRANT
        ),
        name="profits",
    )(
        block_list.T,
        block_owner,
        desk_owner.reshape(1, desks),
        buckets.reshape(n, 1, f_dev),
        loadings.T,
        reduced_shocks.T,
        sensitivity.T,
        cross_gamma,
    )
    profit, shortfall, adjusted = pl.pallas_call(
        functools.partial(write_kernel, tail, desk_dev),
        out_shape=outputs,
        in_specs=[anywhere] * 2,
        out_specs=(anywhere,) * 3,
        scratch_shapes=[
            pltpu.VMEM(outputs[0].shape, F32),
            pltpu.VMEM((n_scen, 2 * LIST, lanes), F32),
            pltpu.VMEM(outputs[1].shape, F32),
            pltpu.VMEM(outputs[2].shape, F32),
            dma((5,)),
        ],
        compiler_params=pltpu.CompilerParams(vmem_limit_bytes=GRANT),
        name="write_results",
    )(*results)
    return jnp.transpose(profit, (1, 0, 2)), shortfall.T, adjusted.reshape(desk_dev)


def solution(mesh):
    return jax.shard_map(
        functools.partial(local_program, mesh.shape["fac"], mesh.shape["scen"]),
        mesh=mesh,
        in_specs=(
            P("fac", None),
            P(None, "scen"),
            P("fac", None),
            P("fac", None, None),
            P(),
            P(),
            P(),
            P(),
        ),
        out_specs=(P("fac", None, "scen"), P("fac", None), P("fac")),
        check_vma=False,
    )
```

```python
import functools

import jax
import jax.numpy as jnp
from jax import lax
from jax.experimental import pallas as pl
from jax.experimental.pallas import tpu as pltpu
from jax.sharding import PartitionSpec as P

HORIZONS = 5
CAP = 2
REACH = 2
WINDOW = 2 * REACH + 1
GROUP = 32
PARTS = 2
PIECES = 2
LANES = 384
GRANT = 63 * 1024 * 1024
LIST = 8
MESH = pl.DeviceIdType.MESH
F32 = jnp.float32
BF16 = jnp.bfloat16

horizon_weights = (1.0, 1.0, 2.0, 2.0, 6.0)


def dot_nt(a, b):
    return lax.dot_general(a, b, (((1,), (1,)), ((), ())), preferred_element_type=F32)


def one_hot(condition):
    return jnp.where(condition, 1.0, 0.0).astype(BF16)


def exchange(items, i, j):
    high, low = jnp.maximum(items[i], items[j]), jnp.minimum(items[i], items[j])
    items[i], items[j] = high, low


SORT8 = (
    (0, 1), (2, 3), (4, 5), (6, 7), (0, 2), (1, 3), (4, 6), (5, 7), (1, 2), (5, 6),
    (0, 4), (1, 5), (2, 6), (3, 7), (2, 4), (3, 5), (1, 2), (3, 4), (5, 6),
)


def merge_sorted(first, second):
    items = [jnp.maximum(first[i], second[LIST - 1 - i]) for i in range(LIST)]
    for stride in (4, 2, 1):
        for i in range(LIST):
            if not i & stride:
                exchange(items, i, i + stride)
    return items


def sorted_tail(losses):
    items = [losses[8 * i : 8 * i + 8] for i in range(LIST)]
    for i, j in SORT8:
        exchange(items, i, j)
    for shift in (4, 2, 1):
        items = merge_sorted(items, [pltpu.roll(item, shift, 0) for item in items])
    return items


def sort_sublanes(tile, sublane, descending):
    for stride in (4, 2, 1):
        first = (sublane & stride) == 0
        other = jnp.where(first, pltpu.roll(tile, 8 - stride, 0), pltpu.roll(tile, stride, 0))
        takes_high = first if descending else jnp.logical_not(first)
        tile = jnp.where(takes_high, jnp.maximum(tile, other), jnp.minimum(tile, other))
    return tile


def write_kernel(
    tail, desk_dev,
    profit, lists_in, profit_out, short_out, adjusted_out, profit_v, lists, short_v, adjusted_v, sem,
):
    read_lists = pltpu.make_async_copy(lists_in, lists, sem.at[0])
    read_profit = pltpu.make_async_copy(profit, profit_v, sem.at[1])
    read_lists.start()
    read_profit.start()
    read_profit.wait()
    writes = [
        pltpu.make_async_copy(source, target, sem.at[2 + i])
        for i, (source, target) in enumerate(
            ((profit_v, profit_out), (short_v, short_out), (adjusted_v, adjusted_out))
        )
    ]
    writes[0].start()
    read_lists.wait()
    sublane = lax.broadcasted_iota(jnp.int32, (LIST, lists.shape[2]), 0)
    first = sort_sublanes(jnp.maximum(lists[0, 0:LIST], lists[1, LIST:]), sublane, True)
    second = sort_sublanes(jnp.maximum(lists[2, 0:LIST], lists[3, LIST:]), sublane, False)
    best = jnp.maximum(first, pltpu.roll(second, tail, 0))
    mean = jnp.sum(jnp.where(sublane < tail, best, 0.0), axis=0, keepdims=True) * (1.0 / tail)
    total = jnp.zeros((1, desk_dev), F32)
    for h in range(HORIZONS):
        row = mean[:, h * GROUP : h * GROUP + desk_dev]
        short_v[h : h + 1, :] = row
        total = total + horizon_weights[h] * row * row
    adjusted_v[...] = jnp.sqrt(total + 1e-06)
    for copy in writes[1:]:
        copy.start()
    for copy in writes:
        copy.wait()


def kernel(
    n, n_scen, desk_dev,
    blist_in, bowner_in, desk_owner_in, buckets_in, loadings, reduced, sensitivity, gamma,
    profit_hbm, lists_hbm, profit_out, out_sem,
    blist, bowner, desk_owner, buckets, lbuf, rbuf, sbuf, gbuf, win, masked, terms, pair_buf, totals, piece_out, piece_in,
    gam, lists,
    local_sem, load_sem, win_send, win_recv, pair_sem, piece_send, piece_recv, gam_send, gam_recv,
    scen_send, scen_recv,
):
    me = lax.axis_index("fac")
    sc = lax.axis_index("scen")
    nh = n // 2
    core, chip = lax.rem(me, 2), me // 2
    s_dev = reduced.shape[0]
    f_dev = loadings.shape[1]
    desks = sensitivity.shape[0]
    blocks = bowner_in.shape[0]
    hs = HORIZONS * s_dev
    part = f_dev // PARTS

    def columns(i):
        return pl.ds(i * part, part)

    load_reduced = pltpu.make_async_copy(reduced, rbuf, local_sem.at[0])
    load_sensitivity = pltpu.make_async_copy(sensitivity, sbuf, local_sem.at[1])
    piece = part // PIECES
    load_loadings = [
        pltpu.make_async_copy(
            loadings.at[:, pl.ds(i * piece, piece)],
            lbuf.at[:, pl.ds(i * piece, piece)],
            load_sem.at[0, i],
        )
        for i in range(PARTS * PIECES)
    ]
    rows_each = f_dev // PIECES
    load_gamma = [
        pltpu.make_async_copy(
            gamma.at[k, pl.ds(i * rows_each, rows_each)],
            gbuf.at[k, pl.ds(i * rows_each, rows_each)],
            load_sem.at[1, k * PIECES + i],
        )
        for k in range(CAP)
        for i in range(PIECES)
    ]
    small = [
        pltpu.make_async_copy(source, target, local_sem.at[2 + i])
        for i, (source, target) in enumerate(
            (
                (desk_owner_in, desk_owner), (buckets_in, buckets),
                (blist_in, blist), (bowner_in, bowner),
            )
        )
    ]
    for copy in [load_reduced] + load_loadings + small:
        copy.start()

    barrier = pltpu.get_barrier_semaphore()
    for step in range(1, n):
        pl.semaphore_signal(
            barrier, inc=1, device_id={"fac": lax.rem(me + step, n)}, device_id_type=MESH
        )
    for step in range(1, n_scen):
        pl.semaphore_signal(
            barrier, inc=1, device_id={"scen": lax.rem(sc + step, n_scen)}, device_id_type=MESH
        )

    partner = me + 1 - 2 * core
    side = 2 * core - 1

    def window_copy(index, from_slot, to_slot, i, target):
        return pltpu.make_async_remote_copy(
            src_ref=win.at[from_slot, i],
            dst_ref=win.at[to_slot, i],
            send_sem=win_send.at[index],
            recv_sem=win_recv.at[to_slot, i],
            device_id={"fac": jnp.clip(target, 0, n - 1)},
            device_id_type=MESH,
        )

    has_both = (chip + side >= 0) & (chip + side < nh)
    has_one = (chip - side >= 0) & (chip - side < nh)
    has_left, has_right = chip > 0, chip < nh - 1

    def to_both(i):
        target = 2 * (chip + side) + i
        return window_copy(i, REACH, REACH + me - target, i, target)

    def to_one(i):
        return window_copy(PARTS + i, REACH, REACH + 2 * side, i, me - 2 * side)

    def to_partner(i):
        return window_copy(2 * PARTS + i, REACH, REACH + me - partner, i, partner)

    left_slot, right_slot = REACH - 1 - core, REACH + 2 - core

    def hand_left():
        return window_copy(3 * PARTS, left_slot, left_slot + me - partner, core, partner)

    def hand_right():
        return window_copy(3 * PARTS + 1, right_slot, right_slot + me - partner, core, partner)

    def arrival(slot, i):
        return pltpu.make_async_remote_copy(
            src_ref=win.at[REACH, i],
            dst_ref=win.at[slot, i],
            send_sem=win_send.at[0],
            recv_sem=win_recv.at[slot, i],
            device_id={"fac": partner},
            device_id_type=MESH,
        )

    load_reduced.wait()
    for i in range(PARTS):
        for copy in load_loadings[i * PIECES : (i + 1) * PIECES]:
            copy.wait()
        if i == PARTS - 1:
            for copy in [load_sensitivity] + load_gamma:
                copy.start()
        win[REACH, i] = jnp.dot(
            rbuf[...], lbuf[:, columns(i)], preferred_element_type=F32
        ).astype(BF16)
        if i == 0:
            pl.semaphore_wait(barrier, n - 1 + n_scen - 1)

        @pl.when(has_both)
        def _(i=i):
            to_both(i).start()

        to_partner(i).start()

    def window(slot):
        return jnp.concatenate([win[slot, i] for i in range(PARTS)], axis=1)

    for copy in small:
        copy.wait()

    owner_row = desk_owner[...]
    owns = one_hot(lax.broadcasted_iota(jnp.int32, (n, desks), 0) == owner_row)
    before = one_hot(
        lax.broadcasted_iota(jnp.int32, (desks, desks), 0)
        < lax.broadcasted_iota(jnp.int32, (desks, desks), 1)
    )
    earlier = jnp.dot(owns, before, preferred_element_type=F32)
    rank_row = jnp.sum(owns.astype(F32) * earlier, axis=0, keepdims=True).astype(jnp.int32)
    slot_row = ((owner_row & 1) * nh + (owner_row >> 1)) * GROUP + rank_row
    my_group = core * nh + chip

    def fill_masked(k, shocks, row):
        for h in range(HORIZONS):
            masked[k, h * s_dev : (h + 1) * s_dev, :] = shocks * one_hot(row >= h)

    fill_masked(CAP, window(REACH), buckets[me])
    load_sensitivity.wait()
    chunk = min(n * GROUP, 256)

    def add_terms(i, carry):
        start = pl.multiple_of(i * chunk, chunk)
        place = one_hot(
            lax.broadcasted_iota(jnp.int32, (chunk, desks), 0) + start == slot_row
        )
        placed = jnp.dot(place, sbuf[...], preferred_element_type=F32).astype(BF16)
        terms[pl.ds(start, chunk), :] = dot_nt(placed, masked[CAP])
        return carry

    lax.fori_loop(0, n * GROUP // chunk, add_terms, 0)

    half = nh * GROUP
    pair = pltpu.make_async_remote_copy(
        src_ref=terms.at[pl.ds(pl.multiple_of((1 - core) * half, half), half)],
        dst_ref=pair_buf,
        send_sem=pair_sem.at[0],
        recv_sem=pair_sem.at[1],
        device_id={"fac": partner},
        device_id_type=MESH,
    )
    pair.start()

    @pl.when(has_one)
    def _():
        for i in range(PARTS):
            to_one(i).start()

    bpad = (blocks + 15) // 16 * 16
    block_ids = lax.broadcasted_iota(jnp.int32, (bpad, 1), 0)

    def read_block(b, carry):
        count, live, rows, cols, owner_col, desk_col = carry
        owner = bowner[b]
        mine = owner == me
        live = tuple(jnp.where(mine & (count == k), 1, live[k]) for k in range(CAP))
        rows = tuple(jnp.where(mine & (count == k), blist[0, b], rows[k]) for k in range(CAP))
        cols = tuple(jnp.where(mine & (count == k), blist[1, b], cols[k]) for k in range(CAP))
        owner_col = jnp.where(block_ids == b, owner, owner_col)
        desk_col = jnp.where(block_ids == b, blist[2, b], desk_col)
        return count + jnp.where(mine, 1, 0), live, rows, cols, owner_col, desk_col

    empty = jnp.full((bpad, 1), -1, jnp.int32)
    zero = jnp.int32(0)
    _, live, rows, cols, owner_col, desk_col = lax.fori_loop(
        0, blocks, read_block, (zero, (zero,) * CAP, (me,) * CAP, (me,) * CAP, empty, empty)
    )
    block_owns = one_hot(owner_col == lax.broadcasted_iota(jnp.int32, (bpad, n), 1))
    above = one_hot(
        lax.broadcasted_iota(jnp.int32, (bpad, bpad), 0)
        > lax.broadcasted_iota(jnp.int32, (bpad, bpad), 1)
    )
    block_earlier = jnp.dot(above, block_owns, preferred_element_type=F32)
    block_rank = jnp.sum(
        block_owns.astype(F32) * block_earlier, axis=1, keepdims=True
    ).astype(jnp.int32)
    distance = me - owner_col
    distance = jnp.where(distance < 0, distance + n, distance)
    key = jnp.where(owner_col >= 0, block_rank * n + distance, -1)
    key_hot = one_hot(key == lax.broadcasted_iota(jnp.int32, (bpad, CAP * n), 1))
    desk_hot = one_hot(desk_col == lax.broadcasted_iota(jnp.int32, (bpad, desks), 1))
    my_desks = one_hot(
        lax.broadcasted_iota(jnp.int32, (GROUP, desks), 0) + my_group * GROUP == slot_row
    )
    gather_rows = jnp.dot(
        dot_nt(my_desks, desk_hot).astype(BF16), key_hot, preferred_element_type=F32
    )

    pair.wait_recv()
    for j in range(nh):
        start = pl.multiple_of(core * half + j * GROUP, GROUP)
        total = terms[pl.ds(start, GROUP), :] + pair_buf[j * GROUP : (j + 1) * GROUP, :]
        totals[j] = total
        piece_out[j] = total.astype(BF16)
    pieces = []
    for step in range(1, nh):
        target = lax.rem(chip + step, nh)
        copy = pltpu.make_async_remote_copy(
            src_ref=piece_out.at[target],
            dst_ref=piece_in.at[step],
            send_sem=piece_send.at[step],
            recv_sem=piece_recv.at[step],
            device_id={"fac": 2 * target + core},
            device_id_type=MESH,
        )
        copy.start()
        pieces.append(copy)

    @pl.when(has_left)
    def _():
        arrival(left_slot, core).wait_recv()
        hand_left().start()

    @pl.when(has_right)
    def _():
        arrival(right_slot, core).wait_recv()
        hand_right().start()

    for i in range(PARTS):
        arrival(REACH + partner - me, i).wait_recv()

        @pl.when(has_both)
        def _(i=i):
            arrival(REACH + 2 * side, i).wait_recv()

    @pl.when(has_left)
    def _():
        arrival(left_slot, 1 - core).wait_recv()

    @pl.when(has_right)
    def _():
        arrival(right_slot, 1 - core).wait_recv()

    for copy in load_gamma:
        copy.wait()
    for k in range(CAP):
        fill_masked(k, window(jnp.clip(cols[k] - me + REACH, 0, WINDOW - 1)), buckets[cols[k]])
    for k in range(CAP):
        row_part = window(jnp.clip(rows[k] - me + REACH, 0, WINDOW - 1)).astype(F32)
        row_bucket = buckets[rows[k]]
        folded = [jnp.zeros((s_dev, 128), F32)] * HORIZONS
        for start in range(0, f_dev, 256):
            product = dot_nt(masked[k], gbuf[k, start : start + 256, :])
            for h in range(HORIZONS):
                for i in (0, 128):
                    at = start + i
                    factor = jnp.where(
                        row_bucket[:, at : at + 128] >= h, row_part[:, at : at + 128], 0.0
                    )
                    folded[h] = folded[h] + factor * product[h * s_dev : (h + 1) * s_dev, i : i + 128]
        quad = jnp.sum(jnp.transpose(jnp.concatenate(folded, axis=0)), axis=0, keepdims=True)
        gam[0, :, k * LANES : k * LANES + hs] = quad * (0.5 * live[k].astype(F32))
    rows_out = []
    for step in range(1, n):
        copy = pltpu.make_async_remote_copy(
            src_ref=gam.at[0],
            dst_ref=gam.at[step],
            send_sem=gam_send.at[step],
            recv_sem=gam_recv.at[step],
            device_id={"fac": lax.rem(me + step, n)},
            device_id_type=MESH,
        )
        copy.start()
        rows_out.append(copy)

    own = totals[chip]
    for step, copy in enumerate(pieces, 1):
        copy.wait_recv()
        own = own + piece_in[step].astype(F32)
    for copy in rows_out:
        copy.wait_recv()
    gamma_rows = jnp.concatenate(
        [gam[q, :, k * LANES : k * LANES + hs] for k in range(CAP) for q in range(n)], axis=0
    )
    own = own + jnp.dot(
        gather_rows, gamma_rows, precision=lax.Precision.HIGHEST, preferred_element_type=F32
    )
    stacked = [own[:, h * s_dev : (h + 1) * s_dev] for h in range(HORIZONS)]
    for h in range(HORIZONS):
        profit_out[h] = stacked[h][0:desk_dev]
    write_profit = pltpu.make_async_copy(profit_out, profit_hbm, out_sem.at[0])
    write_profit.start()
    lanes = lists.shape[1]
    stacked.append(jnp.zeros((lanes - HORIZONS * GROUP, s_dev), F32))
    tall = jnp.concatenate(stacked, axis=0)
    tall = jnp.concatenate([tall, jnp.zeros((lanes, 128 - s_dev), F32)], axis=1)
    items = sorted_tail(-jnp.transpose(tall)[0:s_dev])
    sublane = lax.broadcasted_iota(jnp.int32, (LIST, lanes), 0)
    down, up = items[0], items[LIST - 1]
    for i in range(1, LIST):
        down = jnp.where(sublane == i, items[i], down)
        up = jnp.where(sublane == i, items[LIST - 1 - i], up)
    lists[0:LIST] = down
    lists[LIST : 2 * LIST] = up
    scen_copies = []
    for step in range(1, n_scen):
        copy = pltpu.make_async_remote_copy(
            src_ref=lists,
            dst_ref=lists_hbm.at[step],
            send_sem=scen_send.at[step],
            recv_sem=scen_recv.at[step],
            device_id={"scen": lax.rem(sc + step, n_scen)},
            device_id_type=MESH,
        )
        copy.start()
        scen_copies.append(copy)
    write_lists = pltpu.make_async_copy(lists, lists_hbm.at[0], out_sem.at[1])
    write_lists.start()

    for i in range(PARTS):
        @pl.when(has_both)
        def _(i=i):
            to_both(i).wait_send()

        @pl.when(has_one)
        def _(i=i):
            to_one(i).wait_send()

        to_partner(i).wait_send()

    @pl.when(has_left)
    def _():
        hand_left().wait_send()

    @pl.when(has_right)
    def _():
        hand_right().wait_send()

    pair.wait_send()
    for copy in pieces + rows_out:
        copy.wait_send()
    for copy in scen_copies:
        copy.wait()

    write_profit.wait()
    write_lists.wait()


def local_program(
    n, n_scen,
    loadings, reduced_shocks, sensitivity, cross_gamma, block_list, block_owner, desk_owner, buckets,
):
    f_dev, depth = loadings.shape
    s_dev = reduced_shocks.shape[1]
    desks = sensitivity.shape[1]
    desk_dev = (desks + n - 1) // n + 1
    hs = HORIZONS * s_dev
    nh = n // 2
    tail = (s_dev * n_scen * 25 + 999) // 1000
    lanes = (HORIZONS * GROUP + 127) // 128 * 128
    anywhere = pl.BlockSpec(memory_space=pl.ANY)
    dma = pltpu.SemaphoreType.DMA
    outputs = (
        jax.ShapeDtypeStruct((HORIZONS, desk_dev, s_dev), F32),
        jax.ShapeDtypeStruct((HORIZONS, desk_dev), F32),
        jax.ShapeDtypeStruct((1, desk_dev), F32),
    )
    results = pl.pallas_call(
        functools.partial(kernel, n, n_scen, desk_dev),
        out_shape=(outputs[0], jax.ShapeDtypeStruct((n_scen, 2 * LIST, lanes), F32)),
        in_specs=[anywhere] * 8,
        out_specs=(anywhere,) * 2,
        scratch_shapes=[
            pltpu.VMEM((HORIZONS, desk_dev, s_dev), F32),
            dma((2,)),
            pltpu.SMEM((3, block_owner.shape[0]), jnp.int32),
            pltpu.SMEM((block_owner.shape[0],), jnp.int32),
            pltpu.VMEM((1, desks), jnp.int32),
            pltpu.VMEM((n, 1, f_dev), jnp.int32),
            pltpu.VMEM((depth, f_dev), BF16),
            pltpu.VMEM((s_dev, depth), BF16),
            pltpu.VMEM((desks, f_dev), BF16),
            pltpu.VMEM((CAP, f_dev, f_dev), BF16),
            pltpu.VMEM((WINDOW, PARTS, s_dev, f_dev // PARTS), BF16),
            pltpu.VMEM((CAP + 1, hs, f_dev), BF16),
            pltpu.VMEM((n * GROUP, hs), F32),
            pltpu.VMEM((nh * GROUP, hs), F32),
            pltpu.VMEM((nh, GROUP, hs), F32),
            pltpu.VMEM((nh, GROUP, hs), BF16),
            pltpu.VMEM((nh, GROUP, hs), BF16),
            pltpu.VMEM((n, 1, CAP * LANES), F32),
            pltpu.VMEM((2 * LIST, lanes), F32),
            dma((6,)),
            dma((2, max(PARTS, CAP) * PIECES)),
            dma((3 * PARTS + 2,)),
            dma((WINDOW, PARTS)),
            dma((2,)),
            dma((nh,)),
            dma((nh,)),
            dma((n,)),
            dma((n,)),
            dma((n_scen,)),
            dma((n_scen,)),
        ],
        compiler_params=pltpu.CompilerParams(
            collective_id=0, has_side_effects=True, vmem_limit_bytes=GRANT
        ),
        name="profits",
    )(
        block_list.T,
        block_owner,
        desk_owner.reshape(1, desks),
        buckets.reshape(n, 1, f_dev),
        loadings.T,
        reduced_shocks.T,
        sensitivity.T,
        cross_gamma,
    )
    profit, shortfall, adjusted = pl.pallas_call(
        functools.partial(write_kernel, tail, desk_dev),
        out_shape=outputs,
        in_specs=[anywhere] * 2,
        out_specs=(anywhere,) * 3,
        scratch_shapes=[
            pltpu.VMEM(outputs[0].shape, F32),
            pltpu.VMEM((n_scen, 2 * LIST, lanes), F32),
            pltpu.VMEM(outputs[1].shape, F32),
            pltpu.VMEM(outputs[2].shape, F32),
            dma((5,)),
        ],
        compiler_params=pltpu.CompilerParams(vmem_limit_bytes=GRANT),
        name="write_results",
    )(*results)
    return jnp.transpose(profit, (1, 0, 2)), shortfall.T, adjusted.reshape(desk_dev)


def solution(mesh):
    return jax.shard_map(
        functools.partial(local_program, mesh.shape["fac"], mesh.shape["scen"]),
        mesh=mesh,
        in_specs=(
            P("fac", None),
            P(None, "scen"),
            P("fac", None),
            P("fac", None, None),
            P(),
            P(),
            P(),
            P(),
        ),
        out_specs=(P("fac", None, "scen"), P("fac", None), P("fac")),
        check_vma=False,
    )
```

```python
import functools

import jax
import jax.numpy as jnp
from jax import lax
from jax.experimental import pallas as pl
from jax.experimental.pallas import tpu as pltpu
from jax.sharding import PartitionSpec as P

HORIZONS = 5
CAP = 2
REACH = 2
WINDOW = 2 * REACH + 1
GROUP = 32
PARTS = 2
PIECES = 2
LANES = 384
GRANT = 63 * 1024 * 1024
LIST = 8
MESH = pl.DeviceIdType.MESH
F32 = jnp.float32
BF16 = jnp.bfloat16

horizon_weights = (1.0, 1.0, 2.0, 2.0, 6.0)


def dot_nt(a, b):
    return lax.dot_general(a, b, (((1,), (1,)), ((), ())), preferred_element_type=F32)


def one_hot(condition):
    return jnp.where(condition, 1.0, 0.0).astype(BF16)


def exchange(items, i, j):
    high, low = jnp.maximum(items[i], items[j]), jnp.minimum(items[i], items[j])
    items[i], items[j] = high, low


SORT8 = (
    (0, 1), (2, 3), (4, 5), (6, 7), (0, 2), (1, 3), (4, 6), (5, 7), (1, 2), (5, 6),
    (0, 4), (1, 5), (2, 6), (3, 7), (2, 4), (3, 5), (1, 2), (3, 4), (5, 6),
)


def merge_sorted(first, second):
    items = [jnp.maximum(first[i], second[LIST - 1 - i]) for i in range(LIST)]
    for stride in (4, 2, 1):
        for i in range(LIST):
            if not i & stride:
                exchange(items, i, i + stride)
    return items


def sorted_tail(losses):
    items = [losses[8 * i : 8 * i + 8] for i in range(LIST)]
    for i, j in SORT8:
        exchange(items, i, j)
    for shift in (4, 2, 1):
        items = merge_sorted(items, [pltpu.roll(item, shift, 0) for item in items])
    return items


def sort_sublanes(tile, sublane, descending):
    for stride in (4, 2, 1):
        first = (sublane & stride) == 0
        other = jnp.where(first, pltpu.roll(tile, 8 - stride, 0), pltpu.roll(tile, stride, 0))
        takes_high = first if descending else jnp.logical_not(first)
        tile = jnp.where(takes_high, jnp.maximum(tile, other), jnp.minimum(tile, other))
    return tile


def write_kernel(
    tail, desk_dev,
    profit, lists_in, profit_out, short_out, adjusted_out, profit_v, lists, short_v, adjusted_v, sem,
):
    read_lists = pltpu.make_async_copy(lists_in, lists, sem.at[0])
    read_profit = pltpu.make_async_copy(profit, profit_v, sem.at[1])
    read_lists.start()
    read_profit.start()
    read_profit.wait()
    writes = [
        pltpu.make_async_copy(source, target, sem.at[2 + i])
        for i, (source, target) in enumerate(
            ((profit_v, profit_out), (short_v, short_out), (adjusted_v, adjusted_out))
        )
    ]
    writes[0].start()
    read_lists.wait()
    sublane = lax.broadcasted_iota(jnp.int32, (LIST, lists.shape[2]), 0)
    first = sort_sublanes(jnp.maximum(lists[0, 0:LIST], lists[1, LIST:]), sublane, True)
    second = sort_sublanes(jnp.maximum(lists[2, 0:LIST], lists[3, LIST:]), sublane, False)
    best = jnp.maximum(first, pltpu.roll(second, tail, 0))
    mean = jnp.sum(jnp.where(sublane < tail, best, 0.0), axis=0, keepdims=True) * (1.0 / tail)
    total = jnp.zeros((1, desk_dev), F32)
    for h in range(HORIZONS):
        row = mean[:, h * GROUP : h * GROUP + desk_dev]
        short_v[h : h + 1, :] = row
        total = total + horizon_weights[h] * row * row
    adjusted_v[...] = jnp.sqrt(total + 1e-06)
    for copy in writes[1:]:
        copy.start()
    for copy in writes:
        copy.wait()


def kernel(
    n, n_scen, desk_dev,
    blist_in, bowner_in, desk_owner_in, buckets_in, loadings, reduced, sensitivity, gamma,
    profit_hbm, lists_hbm, profit_out, out_sem,
    blist, bowner, desk_owner, buckets, lbuf, rbuf, sbuf, gbuf, win, masked, terms, pair_buf, totals, piece_out, piece_in,
    gam, lists,
    local_sem, load_sem, win_send, win_recv, pair_sem, piece_send, piece_recv, gam_send, gam_recv,
    scen_send, scen_recv,
):
    me = lax.axis_index("fac")
    sc = lax.axis_index("scen")
    nh = n // 2
    core, chip = lax.rem(me, 2), me // 2
    s_dev = reduced.shape[0]
    f_dev = loadings.shape[1]
    desks = sensitivity.shape[0]
    blocks = bowner_in.shape[0]
    hs = HORIZONS * s_dev
    part = f_dev // PARTS

    def columns(i):
        return pl.ds(i * part, part)

    load_reduced = pltpu.make_async_copy(reduced, rbuf, local_sem.at[0])
    load_sensitivity = pltpu.make_async_copy(sensitivity, sbuf, local_sem.at[1])
    piece = part // PIECES
    load_loadings = [
        pltpu.make_async_copy(
            loadings.at[:, pl.ds(i * piece, piece)],
            lbuf.at[:, pl.ds(i * piece, piece)],
            load_sem.at[0, i],
        )
        for i in range(PARTS * PIECES)
    ]
    rows_each = f_dev // PIECES
    load_gamma = [
        pltpu.make_async_copy(
            gamma.at[k, pl.ds(i * rows_each, rows_each)],
            gbuf.at[k, pl.ds(i * rows_each, rows_each)],
            load_sem.at[1, k * PIECES + i],
        )
        for k in range(CAP)
        for i in range(PIECES)
    ]
    small = [
        pltpu.make_async_copy(source, target, local_sem.at[2 + i])
        for i, (source, target) in enumerate(
            (
                (desk_owner_in, desk_owner), (buckets_in, buckets),
                (blist_in, blist), (bowner_in, bowner),
            )
        )
    ]
    for copy in [load_reduced] + load_loadings + small + [load_sensitivity] + load_gamma:
        copy.start()

    barrier = pltpu.get_barrier_semaphore()
    for step in range(1, n):
        pl.semaphore_signal(
            barrier, inc=1, device_id={"fac": lax.rem(me + step, n)}, device_id_type=MESH
        )
    for step in range(1, n_scen):
        pl.semaphore_signal(
            barrier, inc=1, device_id={"scen": lax.rem(sc + step, n_scen)}, device_id_type=MESH
        )

    partner = me + 1 - 2 * core
    side = 2 * core - 1

    def window_copy(index, from_slot, to_slot, i, target):
        return pltpu.make_async_remote_copy(
            src_ref=win.at[from_slot, i],
            dst_ref=win.at[to_slot, i],
            send_sem=win_send.at[index],
            recv_sem=win_recv.at[to_slot, i],
            device_id={"fac": jnp.clip(target, 0, n - 1)},
            device_id_type=MESH,
        )

    has_both = (chip + side >= 0) & (chip + side < nh)
    has_one = (chip - side >= 0) & (chip - side < nh)
    has_left, has_right = chip > 0, chip < nh - 1

    def to_both(i):
        target = 2 * (chip + side) + i
        return window_copy(i, REACH, REACH + me - target, i, target)

    def to_one(i):
        return window_copy(PARTS + i, REACH, REACH + 2 * side, i, me - 2 * side)

    def to_partner(i):
        return window_copy(2 * PARTS + i, REACH, REACH + me - partner, i, partner)

    left_slot, right_slot = REACH - 1 - core, REACH + 2 - core

    def hand_left():
        return window_copy(3 * PARTS, left_slot, left_slot + me - partner, core, partner)

    def hand_right():
        return window_copy(3 * PARTS + 1, right_slot, right_slot + me - partner, core, partner)

    def arrival(slot, i):
        return pltpu.make_async_remote_copy(
            src_ref=win.at[REACH, i],
            dst_ref=win.at[slot, i],
            send_sem=win_send.at[0],
            recv_sem=win_recv.at[slot, i],
            device_id={"fac": partner},
            device_id_type=MESH,
        )

    load_reduced.wait()
    for i in range(PARTS):
        for copy in load_loadings[i * PIECES : (i + 1) * PIECES]:
            copy.wait()
        win[REACH, i] = jnp.dot(
            rbuf[...], lbuf[:, columns(i)], preferred_element_type=F32
        ).astype(BF16)
        if i == 0:
            pl.semaphore_wait(barrier, n - 1 + n_scen - 1)

        @pl.when(has_both)
        def _(i=i):
            to_both(i).start()

        to_partner(i).start()

    def window(slot):
        return jnp.concatenate([win[slot, i] for i in range(PARTS)], axis=1)

    for copy in small:
        copy.wait()

    owner_row = desk_owner[...]
    owns = one_hot(lax.broadcasted_iota(jnp.int32, (n, desks), 0) == owner_row)
    before = one_hot(
        lax.broadcasted_iota(jnp.int32, (desks, desks), 0)
        < lax.broadcasted_iota(jnp.int32, (desks, desks), 1)
    )
    earlier = jnp.dot(owns, before, preferred_element_type=F32)
    rank_row = jnp.sum(owns.astype(F32) * earlier, axis=0, keepdims=True).astype(jnp.int32)
    slot_row = ((owner_row & 1) * nh + (owner_row >> 1)) * GROUP + rank_row
    my_group = core * nh + chip

    def fill_masked(k, shocks, row):
        for h in range(HORIZONS):
            masked[k, h * s_dev : (h + 1) * s_dev, :] = shocks * one_hot(row >= h)

    fill_masked(CAP, window(REACH), buckets[me])
    load_sensitivity.wait()
    chunk = min(n * GROUP, 256)

    def add_terms(i, carry):
        start = pl.multiple_of(i * chunk, chunk)
        place = one_hot(
            lax.broadcasted_iota(jnp.int32, (chunk, desks), 0) + start == slot_row
        )
        placed = jnp.dot(place, sbuf[...], preferred_element_type=F32).astype(BF16)
        terms[pl.ds(start, chunk), :] = dot_nt(placed, masked[CAP])
        return carry

    lax.fori_loop(0, n * GROUP // chunk, add_terms, 0)

    half = nh * GROUP
    pair = pltpu.make_async_remote_copy(
        src_ref=terms.at[pl.ds(pl.multiple_of((1 - core) * half, half), half)],
        dst_ref=pair_buf,
        send_sem=pair_sem.at[0],
        recv_sem=pair_sem.at[1],
        device_id={"fac": partner},
        device_id_type=MESH,
    )
    pair.start()

    @pl.when(has_one)
    def _():
        for i in range(PARTS):
            to_one(i).start()

    bpad = (blocks + 15) // 16 * 16
    block_ids = lax.broadcasted_iota(jnp.int32, (bpad, 1), 0)

    def read_block(b, carry):
        count, live, rows, cols, owner_col, desk_col = carry
        owner = bowner[b]
        mine = owner == me
        live = tuple(jnp.where(mine & (count == k), 1, live[k]) for k in range(CAP))
        rows = tuple(jnp.where(mine & (count == k), blist[0, b], rows[k]) for k in range(CAP))
        cols = tuple(jnp.where(mine & (count == k), blist[1, b], cols[k]) for k in range(CAP))
        owner_col = jnp.where(block_ids == b, owner, owner_col)
        desk_col = jnp.where(block_ids == b, blist[2, b], desk_col)
        return count + jnp.where(mine, 1, 0), live, rows, cols, owner_col, desk_col

    empty = jnp.full((bpad, 1), -1, jnp.int32)
    zero = jnp.int32(0)
    _, live, rows, cols, owner_col, desk_col = lax.fori_loop(
        0, blocks, read_block, (zero, (zero,) * CAP, (me,) * CAP, (me,) * CAP, empty, empty)
    )
    block_owns = one_hot(owner_col == lax.broadcasted_iota(jnp.int32, (bpad, n), 1))
    above = one_hot(
        lax.broadcasted_iota(jnp.int32, (bpad, bpad), 0)
        > lax.broadcasted_iota(jnp.int32, (bpad, bpad), 1)
    )
    block_earlier = jnp.dot(above, block_owns, preferred_element_type=F32)
    block_rank = jnp.sum(
        block_owns.astype(F32) * block_earlier, axis=1, keepdims=True
    ).astype(jnp.int32)
    distance = me - owner_col
    distance = jnp.where(distance < 0, distance + n, distance)
    key = jnp.where(owner_col >= 0, block_rank * n + distance, -1)
    key_hot = one_hot(key == lax.broadcasted_iota(jnp.int32, (bpad, CAP * n), 1))
    desk_hot = one_hot(desk_col == lax.broadcasted_iota(jnp.int32, (bpad, desks), 1))
    my_desks = one_hot(
        lax.broadcasted_iota(jnp.int32, (GROUP, desks), 0) + my_group * GROUP == slot_row
    )
    gather_rows = jnp.dot(
        dot_nt(my_desks, desk_hot).astype(BF16), key_hot, preferred_element_type=F32
    )

    pair.wait_recv()
    for j in range(nh):
        start = pl.multiple_of(core * half + j * GROUP, GROUP)
        total = terms[pl.ds(start, GROUP), :] + pair_buf[j * GROUP : (j + 1) * GROUP, :]
        totals[j] = total
        piece_out[j] = total.astype(BF16)
    pieces = []
    for step in range(1, nh):
        target = lax.rem(chip + step, nh)
        copy = pltpu.make_async_remote_copy(
            src_ref=piece_out.at[target],
            dst_ref=piece_in.at[step],
            send_sem=piece_send.at[step],
            recv_sem=piece_recv.at[step],
            device_id={"fac": 2 * target + core},
            device_id_type=MESH,
        )
        copy.start()
        pieces.append(copy)

    @pl.when(has_left)
    def _():
        arrival(left_slot, core).wait_recv()
        hand_left().start()

    @pl.when(has_right)
    def _():
        arrival(right_slot, core).wait_recv()
        hand_right().start()

    for i in range(PARTS):
        arrival(REACH + partner - me, i).wait_recv()

        @pl.when(has_both)
        def _(i=i):
            arrival(REACH + 2 * side, i).wait_recv()

    @pl.when(has_left)
    def _():
        arrival(left_slot, 1 - core).wait_recv()

    @pl.when(has_right)
    def _():
        arrival(right_slot, 1 - core).wait_recv()

    for copy in load_gamma:
        copy.wait()
    for k in range(CAP):
        fill_masked(k, window(jnp.clip(cols[k] - me + REACH, 0, WINDOW - 1)), buckets[cols[k]])
    for k in range(CAP):
        row_part = window(jnp.clip(rows[k] - me + REACH, 0, WINDOW - 1)).astype(F32)
        row_bucket = buckets[rows[k]]
        folded = [jnp.zeros((s_dev, 128), F32)] * HORIZONS
        for start in range(0, f_dev, 256):
            product = dot_nt(masked[k], gbuf[k, start : start + 256, :])
            for h in range(HORIZONS):
                for i in (0, 128):
                    at = start + i
                    factor = jnp.where(
                        row_bucket[:, at : at + 128] >= h, row_part[:, at : at + 128], 0.0
                    )
                    folded[h] = folded[h] + factor * product[h * s_dev : (h + 1) * s_dev, i : i + 128]
        quad = jnp.sum(jnp.transpose(jnp.concatenate(folded, axis=0)), axis=0, keepdims=True)
        gam[0, :, k * LANES : k * LANES + hs] = quad * (0.5 * live[k].astype(F32))
    rows_out = []
    for step in range(1, n):
        copy = pltpu.make_async_remote_copy(
            src_ref=gam.at[0],
            dst_ref=gam.at[step],
            send_sem=gam_send.at[step],
            recv_sem=gam_recv.at[step],
            device_id={"fac": lax.rem(me + step, n)},
            device_id_type=MESH,
        )
        copy.start()
        rows_out.append(copy)

    own = totals[chip]
    for step, copy in enumerate(pieces, 1):
        copy.wait_recv()
        own = own + piece_in[step].astype(F32)
    for copy in rows_out:
        copy.wait_recv()
    gamma_rows = jnp.concatenate(
        [gam[q, :, k * LANES : k * LANES + hs] for k in range(CAP) for q in range(n)], axis=0
    )
    own = own + jnp.dot(
        gather_rows, gamma_rows, precision=lax.Precision.HIGHEST, preferred_element_type=F32
    )
    stacked = [own[:, h * s_dev : (h + 1) * s_dev] for h in range(HORIZONS)]
    for h in range(HORIZONS):
        profit_out[h] = stacked[h][0:desk_dev]
    write_profit = pltpu.make_async_copy(profit_out, profit_hbm, out_sem.at[0])
    write_profit.start()
    lanes = lists.shape[1]
    stacked.append(jnp.zeros((lanes - HORIZONS * GROUP, s_dev), F32))
    tall = jnp.concatenate(stacked, axis=0)
    tall = jnp.concatenate([tall, jnp.zeros((lanes, 128 - s_dev), F32)], axis=1)
    items = sorted_tail(-jnp.transpose(tall)[0:s_dev])
    sublane = lax.broadcasted_iota(jnp.int32, (LIST, lanes), 0)
    down, up = items[0], items[LIST - 1]
    for i in range(1, LIST):
        down = jnp.where(sublane == i, items[i], down)
        up = jnp.where(sublane == i, items[LIST - 1 - i], up)
    lists[0:LIST] = down
    lists[LIST : 2 * LIST] = up
    scen_copies = []
    for step in range(1, n_scen):
        copy = pltpu.make_async_remote_copy(
            src_ref=lists,
            dst_ref=lists_hbm.at[step],
            send_sem=scen_send.at[step],
            recv_sem=scen_recv.at[step],
            device_id={"scen": lax.rem(sc + step, n_scen)},
            device_id_type=MESH,
        )
        copy.start()
        scen_copies.append(copy)
    write_lists = pltpu.make_async_copy(lists, lists_hbm.at[0], out_sem.at[1])
    write_lists.start()

    for i in range(PARTS):
        @pl.when(has_both)
        def _(i=i):
            to_both(i).wait_send()

        @pl.when(has_one)
        def _(i=i):
            to_one(i).wait_send()

        to_partner(i).wait_send()

    @pl.when(has_left)
    def _():
        hand_left().wait_send()

    @pl.when(has_right)
    def _():
        hand_right().wait_send()

    pair.wait_send()
    for copy in pieces + rows_out:
        copy.wait_send()
    for copy in scen_copies:
        copy.wait()

    write_profit.wait()
    write_lists.wait()


def local_program(
    n, n_scen,
    loadings, reduced_shocks, sensitivity, cross_gamma, block_list, block_owner, desk_owner, buckets,
):
    f_dev, depth = loadings.shape
    s_dev = reduced_shocks.shape[1]
    desks = sensitivity.shape[1]
    desk_dev = (desks + n - 1) // n + 1
    hs = HORIZONS * s_dev
    nh = n // 2
    tail = (s_dev * n_scen * 25 + 999) // 1000
    lanes = (HORIZONS * GROUP + 127) // 128 * 128
    anywhere = pl.BlockSpec(memory_space=pl.ANY)
    dma = pltpu.SemaphoreType.DMA
    outputs = (
        jax.ShapeDtypeStruct((HORIZONS, desk_dev, s_dev), F32),
        jax.ShapeDtypeStruct((HORIZONS, desk_dev), F32),
        jax.ShapeDtypeStruct((1, desk_dev), F32),
    )
    results = pl.pallas_call(
        functools.partial(kernel, n, n_scen, desk_dev),
        out_shape=(outputs[0], jax.ShapeDtypeStruct((n_scen, 2 * LIST, lanes), F32)),
        in_specs=[anywhere] * 8,
        out_specs=(anywhere,) * 2,
        scratch_shapes=[
            pltpu.VMEM((HORIZONS, desk_dev, s_dev), F32),
            dma((2,)),
            pltpu.SMEM((3, block_owner.shape[0]), jnp.int32),
            pltpu.SMEM((block_owner.shape[0],), jnp.int32),
            pltpu.VMEM((1, desks), jnp.int32),
            pltpu.VMEM((n, 1, f_dev), jnp.int32),
            pltpu.VMEM((depth, f_dev), BF16),
            pltpu.VMEM((s_dev, depth), BF16),
            pltpu.VMEM((desks, f_dev), BF16),
            pltpu.VMEM((CAP, f_dev, f_dev), BF16),
            pltpu.VMEM((WINDOW, PARTS, s_dev, f_dev // PARTS), BF16),
            pltpu.VMEM((CAP + 1, hs, f_dev), BF16),
            pltpu.VMEM((n * GROUP, hs), F32),
            pltpu.VMEM((nh * GROUP, hs), F32),
            pltpu.VMEM((nh, GROUP, hs), F32),
            pltpu.VMEM((nh, GROUP, hs), BF16),
            pltpu.VMEM((nh, GROUP, hs), BF16),
            pltpu.VMEM((n, 1, CAP * LANES), F32),
            pltpu.VMEM((2 * LIST, lanes), F32),
            dma((6,)),
            dma((2, max(PARTS, CAP) * PIECES)),
            dma((3 * PARTS + 2,)),
            dma((WINDOW, PARTS)),
            dma((2,)),
            dma((nh,)),
            dma((nh,)),
            dma((n,)),
            dma((n,)),
            dma((n_scen,)),
            dma((n_scen,)),
        ],
        compiler_params=pltpu.CompilerParams(
            collective_id=0, has_side_effects=True, vmem_limit_bytes=GRANT
        ),
        name="profits",
    )(
        block_list.T,
        block_owner,
        desk_owner.reshape(1, desks),
        buckets.reshape(n, 1, f_dev),
        loadings.T,
        reduced_shocks.T,
        sensitivity.T,
        cross_gamma,
    )
    profit, shortfall, adjusted = pl.pallas_call(
        functools.partial(write_kernel, tail, desk_dev),
        out_shape=outputs,
        in_specs=[anywhere] * 2,
        out_specs=(anywhere,) * 3,
        scratch_shapes=[
            pltpu.VMEM(outputs[0].shape, F32),
            pltpu.VMEM((n_scen, 2 * LIST, lanes), F32),
            pltpu.VMEM(outputs[1].shape, F32),
            pltpu.VMEM(outputs[2].shape, F32),
            dma((5,)),
        ],
        compiler_params=pltpu.CompilerParams(vmem_limit_bytes=GRANT),
        name="write_results",
    )(*results)
    return jnp.transpose(profit, (1, 0, 2)), shortfall.T, adjusted.reshape(desk_dev)


def solution(mesh):
    return jax.shard_map(
        functools.partial(local_program, mesh.shape["fac"], mesh.shape["scen"]),
        mesh=mesh,
        in_specs=(
            P("fac", None),
            P(None, "scen"),
            P("fac", None),
            P("fac", None, None),
            P(),
            P(),
            P(),
            P(),
        ),
        out_specs=(P("fac", None, "scen"), P("fac", None), P("fac")),
        check_vma=False,
    )
```
